512 devices in a mesh: dp: 128 (over x_hi, z, y), fsdp: 4 (over x_lo, core).
Axes of the slice: x: 4 (x_hi: 2, x_lo: 2; x = x_hi * 2 + x_lo), y: 4, z: 16, core: 2. Of those that a mesh axis runs over, the one named last changes fastest.
Arguments:
- layer_input: bfloat16 [65536, 2048], P(('dp', 'fsdp')), may hold values from -1.1953125 to 1.1953125
- queries: bfloat16 [65536, 2048], P(('dp', 'fsdp')), may hold values from -16 to 16
- key_vectors: bfloat16 [65536, 2048], P(('dp', 'fsdp')), may hold values from -16 to 16
- value_vectors: bfloat16 [65536, 2048], P(('dp', 'fsdp')), may hold values from -6 to 6
- output_grad: bfloat16 [65536, 2048], P(('dp', 'fsdp')), may hold values from -96 to 96
- partner_offsets: int32 [128, 2], P('dp'), may hold values from -2 to 2, as said below
Outputs:
- weight_grad: bfloat16 [128, 2048, 2048], P('dp', 'fsdp')
- value_grad: bfloat16 [65536, 2048], P(('dp', 'fsdp'))
The draws below stay inside these ranges and needn't reach their ends.
Inputs may be any that keep to these rules, and one draw needn't show every extreme that they name: `partner_offsets`: each replica's 2 offsets are distinct and nonzero.
All inputs are finite; a program needn't handle non-finite values.
Results may differ from the reference program's by a relative error of at most 0.0086.
Values may be sent and summed in bfloat16 or wider, within the bound.
No kernel may reach another device: no remote copies, remote signals or barrier semaphores. Data moves between devices by JAX's collectives and lax.ppermute only.
A program may use at most 64 MiB of HBM per device.

```python
import jax
import jax.numpy as jnp
from jax import lax

HD = 128
HEADS = 16
DW = 2048
ROWS = 128
HOPS = 2
PARTNERS = 2
HW = 2048
REPLICAS = 128
TOKENS = 65536
N_FSDP = 4


def draw_queries(key, part):
    key = jax.random.fold_in(key, 5)
    result = jnp.clip(jax.random.normal(key, (TOKENS, HW), jnp.float32), -6.0, 6.0)
    return result.astype(jnp.bfloat16)


def draw_key_vectors(key, part):
    key = jax.random.fold_in(key, 6)
    result = jnp.clip(jax.random.normal(key, (TOKENS, HW), jnp.float32), -6.0, 6.0)
    return result.astype(jnp.bfloat16)


def draw_partner_offsets(key, part):
    key = jax.random.fold_in(key, 7)
    first_key, second_key = jax.random.split(key)
    candidates = 2 * HOPS
    column = jnp.arange(candidates, dtype=jnp.int32)[None, :]
    replica_index = jnp.arange(REPLICAS, dtype=jnp.int32)[:, None]
    scores = jax.random.randint(first_key, (REPLICAS, candidates), 0, 1 << 20, dtype=jnp.int32) * candidates + column
    chosen = jax.random.randint(second_key, (), 0, REPLICAS, dtype=jnp.int32)
    forced = (replica_index == chosen) & ((column == HOPS - 1) | (column == candidates - 1))
    scores = jnp.where(forced, column - candidates, scores)
    ranked = jnp.argsort(scores, axis=1)[:, :PARTNERS].astype(jnp.int32)
    return jnp.where(ranked < HOPS, ranked + 1, HOPS - 1 - ranked).astype(jnp.int32)


def steps_of(own_key, dims, pieces, low, largest):
    gain = 1.0
    for axis_at, parts in pieces:
        draws = jax.random.uniform(jax.random.fold_in(jax.random.fold_in(own_key, 6), axis_at), (parts,), jnp.float32, low / len(pieces), largest / len(pieces))
        gain = gain * jnp.repeat(jnp.exp(draws), dims[axis_at] // parts).reshape((-1,) + (1,) * (len(dims) - 1 - axis_at))
    return gain


def bell_draw(key, shape, scale, bound, cuts=(), kind=jnp.bfloat16):
    factor_of = steps_of(key, shape, cuts, -0.22, 0.18) if cuts else 1.0
    drawn = jax.random.normal(key, shape, jnp.float32) * scale * factor_of
    return jnp.minimum(jnp.maximum(drawn, -bound), bound).astype(kind)


def setup_inputs(seed: int = 0) -> dict:
    streams_of = jax.random.split(jax.random.key(seed), 7)
    layer_input = bell_draw(streams_of[0], (TOKENS, DW), 0.2, 1.1953125, ((0, 512),))
    queries = draw_queries(jax.random.fold_in(streams_of[6], 71), 0)
    key_vectors = draw_key_vectors(jax.random.fold_in(streams_of[6], 71), 0)
    value_vectors = bell_draw(streams_of[3], (TOKENS, HW), 1.0, 6.0, ((0, 512),))
    output_grad = bell_draw(streams_of[4], (TOKENS, HW), 16.0, 96.0, ((0, 512),))
    partner_offsets = draw_partner_offsets(jax.random.fold_in(streams_of[6], 71), 0)
    return dict(layer_input=layer_input, queries=queries, key_vectors=key_vectors, value_vectors=value_vectors, output_grad=output_grad, partner_offsets=partner_offsets)


def rounded_bf(values):
    return lax.optimization_barrier(values.astype(jnp.bfloat16)).astype(jnp.float32)


def reference(layer_input, queries, key_vectors, value_vectors, output_grad, partner_offsets):
    scaling = HD ** -0.5
    split_shape = (REPLICAS, N_FSDP, ROWS, HEADS, HD)
    query_all = queries.reshape(split_shape)
    key_all = key_vectors.reshape(split_shape)
    value_all = value_vectors.reshape(split_shape)
    grads_all = output_grad.reshape(split_shape)
    causal = jnp.arange(ROWS)[None, :] <= jnp.arange(ROWS)[:, None]
    allowed = jnp.concatenate([causal, jnp.ones((ROWS, PARTNERS * ROWS), dtype=bool)], 1)
    hop_list = []
    for stride in range(1, HOPS + 1):
        hop_list = hop_list + [stride, -stride]
    hop_values = jnp.array(hop_list, dtype=jnp.int32)
    window = 2 * HOPS + 1

    def source_parts(replica):
        owners = ((replica + partner_offsets[replica]) % REPLICAS).astype(jnp.int32)
        query_block = query_all[replica].astype(jnp.float32)
        grads_block = grads_all[replica].astype(jnp.float32)
        key_block = jnp.concatenate([key_all[replica][None], key_all[owners]], 0)
        value_block = jnp.concatenate([value_all[replica][None], value_all[owners]], 0)
        key_block = key_block.transpose(1, 0, 2, 3, 4).reshape(N_FSDP, (1 + PARTNERS) * ROWS, HEADS, HD).astype(jnp.float32)
        value_block = value_block.transpose(1, 0, 2, 3, 4).reshape(N_FSDP, (1 + PARTNERS) * ROWS, HEADS, HD).astype(jnp.float32)
        scores = jnp.einsum('fqhd,fkhd->fhqk', query_block, key_block) * scaling
        scores = jnp.where(allowed, scores, -jnp.inf)
        probs = jax.nn.softmax(scores, axis=-1)
        probs_bf = rounded_bf(probs)
        attended = jnp.einsum('fhqk,fkhd->fqhd', probs_bf, value_block)
        row_delta = jnp.sum(grads_block * attended, -1).transpose(0, 2, 1)
        prob_grad = jnp.einsum('fqhd,fkhd->fhqk', grads_block, value_block)
        score_grad = rounded_bf(probs * (prob_grad - row_delta[..., None]) * scaling)
        key_part = jnp.einsum('fhqk,fqhd->fkhd', score_grad, query_block)
        value_part = jnp.einsum('fhqk,fqhd->fkhd', probs_bf, grads_block)
        key_part = key_part.reshape(N_FSDP, 1 + PARTNERS, ROWS, HEADS, HD).transpose(1, 0, 2, 3, 4)
        value_part = value_part.reshape(N_FSDP, 1 + PARTNERS, ROWS, HEADS, HD).transpose(1, 0, 2, 3, 4)
        own = jnp.stack([key_part[0], value_part[0]])
        partner = rounded_bf(jnp.stack([key_part[1:], value_part[1:]], 1))
        match = partner_offsets[replica][:, None] == hop_values[None, :]
        by_hop = jnp.sum(jnp.where(match[:, :, None, None, None, None, None], partner[:, None], 0.0), 0)
        return own, by_hop.astype(jnp.bfloat16)

    def step(carry, moment):
        own_buf, hop_buf = carry
        source = ((moment - HOPS) % REPLICAS).astype(jnp.int32)
        own, by_hop = source_parts(source)
        slot = (moment % window).astype(jnp.int32)
        own_buf = own_buf.at[slot].set(own)
        hop_buf = hop_buf.at[slot].set(by_hop)

        def chain(sign, column_offset):
            def entry(stride):
                place = ((moment - HOPS - sign * stride) % window).astype(jnp.int32)
                return hop_buf[place, 2 * (stride - 1) + column_offset].astype(jnp.float32)
            running = entry(HOPS)
            for stride in range(HOPS - 1, 0, -1):
                running = rounded_bf(running + entry(stride))
            return running

        centre = ((moment - HOPS) % window).astype(jnp.int32)
        total = own_buf[centre] + chain(1, 0) + chain(-1, 1)
        return (own_buf, hop_buf), total.astype(jnp.bfloat16)

    own_empty = jnp.zeros((window, 2, N_FSDP, ROWS, HEADS, HD), jnp.float32)
    hop_empty = jnp.zeros((window, 2 * HOPS, 2, N_FSDP, ROWS, HEADS, HD), jnp.bfloat16)
    _, totals = lax.scan(step, (own_empty, hop_empty), jnp.arange(REPLICAS + 2 * HOPS, dtype=jnp.int32))
    totals = totals[2 * HOPS:]
    value_grad = totals[:, 1].reshape(TOKENS, HW)
    key_grad = totals[:, 0].reshape(REPLICAS, N_FSDP * ROWS, HW)
    inputs_split = layer_input.reshape(REPLICAS, N_FSDP * ROWS, DW)

    def grad_one(operands):
        inputs_part, grads_part = operands
        product = lax.dot_general(inputs_part, grads_part, (((0,), (0,)), ((), ())), preferred_element_type=jnp.float32)
        return product.astype(jnp.bfloat16)

    weight_grad = lax.map(grad_one, (inputs_split, key_grad))
    return weight_grad, value_grad
```

```python
import functools

import jax
import jax.numpy as jnp
from jax import lax
from jax.experimental import pallas as pl
from jax.experimental.pallas import tpu as pltpu
from jax.sharding import PartitionSpec as P

HD = 128
DOCS = (0, 1, -1, 2, -2)
HOPS = 2
GROUP = 4
STEP = 4
TILE = 8
FAR = 1e30


def shifted(value, axis, steps):
    count = lax.axis_size(axis)
    pairs = [(source, (source + steps) % count) for source in range(count)]
    return lax.ppermute(value, axis, pairs)


def swapped(value, axis, mask):
    pairs = [(source, source ^ mask) for source in range(lax.axis_size(axis))]
    return lax.ppermute(value, axis, pairs)


def dot_nt(a, b):
    return lax.dot_general(a, b, (((1,), (1,)), ((), ())), preferred_element_type=jnp.float32)


def dot_nn(a, b):
    return lax.dot_general(a, b, (((1,), (0,)), ((), ())), preferred_element_type=jnp.float32)


def scores_of(keys, query_rows):
    scores = dot_nt(keys, query_rows) * (HD ** (-0.5))
    rows = keys.shape[0]
    own = scores[:, :rows]
    key_at = lax.broadcasted_iota(jnp.int32, own.shape, 0)
    query_at = lax.broadcasted_iota(jnp.int32, own.shape, 1)
    own = jnp.where(key_at <= query_at, own, -FAR)
    return jnp.concatenate([own, scores[:, rows:]], 1)


def head_rows(refs, head):
    return jnp.concatenate([ref[:, head * HD : (head + 1) * HD] for ref in refs], 0)


def stats_kernel(offsets_ref, keys_ref, values_ref, *refs):
    count = len(DOCS)
    query_refs, grad_refs, out_ref = refs[:count], refs[count : 2 * count], refs[2 * count]
    rows = keys_ref.shape[0]
    step = pl.program_id(0)
    base = pl.multiple_of(step * (count * TILE), TILE)
    for head in range(STEP):
        cols = slice(head * HD, (head + 1) * HD)
        scores = scores_of(keys_ref[:, cols], head_rows(query_refs, head))
        prob_grad = dot_nt(values_ref[:, cols], head_rows(grad_refs, head))
        top = jnp.max(scores, 0, keepdims=True)
        weights = jnp.exp(scores - top)
        total = jnp.sum(weights, 0, keepdims=True)
        mean = jnp.sum(weights * prob_grad, 0, keepdims=True) / total
        lse = top + jnp.log(total)
        for doc in range(count):
            cut = slice(doc * rows, (doc + 1) * rows)
            out_ref[pl.ds(base + doc * TILE + head, 1), :] = lse[:, cut]
            out_ref[pl.ds(base + doc * TILE + STEP + head, 1), :] = mean[:, cut]

    @pl.when(step == 0)
    def _():
        tail = out_ref.shape[0] - TILE
        for slot in range(2):
            value = offsets_ref[0, slot].astype(jnp.float32)
            low = tail + slot * STEP
            out_ref[low : low + STEP, :] = jnp.full((STEP, rows), value, jnp.float32)


def merged(stat_refs, me, step, stride):
    def tile(place, row):
        start = pl.multiple_of(place * stride + row, TILE)
        return stat_refs[pl.ds(start, TILE), :]

    count = len(DOCS)
    lse_rows, delta_rows = [], []
    for doc in DOCS:
        owner = me + GROUP + doc
        offsets = tile(owner, stride - TILE)
        first, second = offsets[:STEP], offsets[STEP:]
        parts = []
        for hop in DOCS:
            low = step * (count * TILE) + DOCS.index(-hop) * TILE
            stat = tile(owner + hop, low)
            lse, mean = stat[:STEP], stat[STEP:]
            if hop:
                lse = jnp.where((first == hop) | (second == hop), lse, -FAR)
            parts.append((lse, mean))
        top = functools.reduce(jnp.maximum, [lse for lse, _ in parts])
        weights = [jnp.exp(lse - top) for lse, _ in parts]
        total = sum(weights)
        delta = sum(weight * mean for weight, (_, mean) in zip(weights, parts)) / total
        lse = top + jnp.log(total)
        if doc:
            lse = jnp.where((first == -doc) | (second == -doc), lse, FAR)
        lse_rows.append(lse)
        delta_rows.append(delta)
    return jnp.concatenate(lse_rows, 1), jnp.concatenate(delta_rows, 1)


def grads_kernel(first_step, place_ref, stat_ref, keys_ref, values_ref, *refs):
    count = len(DOCS)
    query_refs, grad_refs = refs[:count], refs[count : 2 * count]
    key_out, value_out = refs[2 * count :]
    step = pl.program_id(0) + first_step
    stride = stat_ref.shape[0] // (3 * GROUP)
    lse, delta = merged(stat_ref, place_ref[0], step, stride)
    for head in range(STEP):
        cols = slice(head * HD, (head + 1) * HD)
        query_rows = head_rows(query_refs, head)
        grad_rows = head_rows(grad_refs, head)
        scores = scores_of(keys_ref[:, cols], query_rows)
        prob_grad = dot_nt(values_ref[:, cols], grad_rows)
        probs = jnp.exp(scores - lse[head : head + 1])
        score_grad = probs * (prob_grad - delta[head : head + 1]) * (HD ** (-0.5))
        key_total = dot_nn(score_grad.astype(jnp.bfloat16), query_rows)
        value_total = dot_nn(probs.astype(jnp.bfloat16), grad_rows)
        key_out[:, cols] = key_total.astype(jnp.bfloat16)
        value_out[:, cols] = value_total.astype(jnp.bfloat16)


def weight_kernel(inputs_ref, *refs):
    grads = jnp.concatenate([ref[...] for ref in refs[:-1]], 0)
    refs[-1][...] = dot_nn(inputs_ref[...], grads).astype(jnp.bfloat16)


def local(layer_input, queries, key_vectors, value_vectors, output_grad, partner_offsets):
    rows, features = queries.shape
    steps = features // (HD * STEP)
    wide = STEP * HD
    mine = lax.axis_index("fsdp")
    places = lax.axis_size("fsdp")
    inputs_all = lax.all_gather(layer_input, "fsdp", axis=0, tiled=True)

    by_doc = {0: (queries, output_grad)}
    up_q, down_q = shifted(queries, "dp", -1), shifted(queries, "dp", 1)
    up_g, down_g = shifted(output_grad, "dp", -1), shifted(output_grad, "dp", 1)
    by_doc[1], by_doc[-1] = (up_q, up_g), (down_q, down_g)
    by_doc[2] = shifted(up_q, "dp", -1), shifted(up_g, "dp", -1)
    by_doc[-2] = shifted(down_q, "dp", 1), shifted(down_g, "dp", 1)
    query_docs = [by_doc[doc][0] for doc in DOCS]
    grad_docs = [by_doc[doc][1] for doc in DOCS]

    width = layer_input.shape[1] // places
    grad_docs[-1], inputs_all = lax.optimization_barrier((grad_docs[-1], inputs_all))
    columns = lax.dynamic_slice_in_dim(inputs_all, mine * width, width, 1)
    columns = columns.reshape(places, rows, width)
    columns = jnp.concatenate(
        [lax.dynamic_index_in_dim(columns, mine ^ k, 0, False) for k in range(places)], 0
    )
    columns = columns.T

    block = pl.BlockSpec((rows, wide), lambda step: (0, step))
    docs = len(DOCS)
    stat_rows = steps * docs * TILE + TILE
    pair = rows * rows * docs * HD * 2
    stats = pl.pallas_call(
        stats_kernel,
        grid=(steps,),
        in_specs=[pl.BlockSpec(memory_space=pltpu.SMEM)] + [block] * (2 + 2 * docs),
        out_specs=pl.BlockSpec((stat_rows, rows), lambda step: (0, 0)),
        out_shape=jax.ShapeDtypeStruct((stat_rows, rows), jnp.float32),
        compiler_params=pltpu.CompilerParams(vmem_limit_bytes=40 << 20),
        cost_estimate=pl.CostEstimate(
            flops=2 * pair * features // HD,
            bytes_accessed=12 * rows * features * 2,
            transcendentals=rows * rows * docs * features // HD,
        ),
        name="stats",
    )(partner_offsets, key_vectors, value_vectors, *query_docs, *grad_docs)

    replicas = lax.axis_size("dp")
    groups = [list(range(low, low + GROUP)) for low in range(0, replicas, GROUP)]
    here = lax.all_gather(stats, "dp", axis=0, tiled=True, axis_index_groups=groups)
    below = shifted(here, "dp", GROUP)
    above = shifted(here, "dp", -GROUP)
    stat_all = jnp.concatenate([below, here, above], 0)
    place = (lax.axis_index("dp") % GROUP).astype(jnp.int32).reshape(1)

    halves = 2
    each = steps // halves
    key_parts, value_parts = [], []
    for half in range(halves):
        low = half * each
        shifted_block = pl.BlockSpec((rows, wide), lambda step, low=low: (0, step + low))
        key_grad, value_grad = pl.pallas_call(
            functools.partial(grads_kernel, low),
            grid=(each,),
            in_specs=[
                pl.BlockSpec(memory_space=pltpu.SMEM),
                pl.BlockSpec(stat_all.shape, lambda step: (0, 0)),
            ]
            + [shifted_block] * (2 + 2 * docs),
            out_specs=[block] * 2,
            out_shape=[jax.ShapeDtypeStruct((rows, each * wide), jnp.bfloat16)] * 2,
            compiler_params=pltpu.CompilerParams(vmem_limit_bytes=40 << 20),
            cost_estimate=pl.CostEstimate(
                flops=4 * pair * features // HD // halves,
                bytes_accessed=14 * rows * features * 2 // halves,
                transcendentals=rows * rows * docs * features // HD // halves,
            ),
            name="grads",
        )(place, stat_all, key_vectors, value_vectors, *query_docs, *grad_docs)
        key_parts.append(key_grad)
        value_parts.append(value_grad)

    weight = None
    full = jax.ShapeDtypeStruct((width, features), jnp.bfloat16)
    for half in range(halves):
        own = key_parts[half]
        across = swapped(own, "fsdp", 2)
        pieces = [own, swapped(own, "fsdp", 1), across, swapped(across, "fsdp", 1)]
        low = half * each
        extra, alias = [], {}
        if weight is not None:
            extra, alias = [weight], {1 + len(pieces): 0}

        def body(inputs_ref, *refs, count=len(pieces)):
            weight_kernel(inputs_ref, *refs[:count], refs[-1])

        weight = pl.pallas_call(
            body,
            grid=(each,),
            in_specs=[pl.BlockSpec(columns.shape, lambda step: (0, 0))]
            + [block] * len(pieces)
            + [pl.BlockSpec(memory_space=pl.ANY)] * len(extra),
            out_specs=pl.BlockSpec((width, wide), lambda step, low=low: (0, step + low)),
            out_shape=full,
            input_output_aliases=alias,
            compiler_params=pltpu.CompilerParams(vmem_limit_bytes=40 << 20),
            cost_estimate=pl.CostEstimate(
                flops=2 * width * columns.shape[1] * each * wide,
                bytes_accessed=2 * each * wide * (columns.shape[1] + width),
                transcendentals=0,
            ),
            name="weight",
        )(columns, *pieces, *extra)
    return weight[None], jnp.concatenate(value_parts, 1)


def solution(mesh):
    return jax.shard_map(
        local,
        mesh=mesh,
        in_specs=(
            P(("dp", "fsdp"), None),
            P(("dp", "fsdp"), None),
            P(("dp", "fsdp"), None),
            P(("dp", "fsdp"), None),
            P(("dp", "fsdp"), None),
            P("dp", None),
        ),
        out_specs=(P("dp", "fsdp", None), P(("dp", "fsdp"), None)),
        check_vma=False,
    )
```

```python
import functools

import jax
import jax.numpy as jnp
from jax import lax
from jax.experimental import pallas as pl
from jax.experimental.pallas import tpu as pltpu
from jax.sharding import PartitionSpec as P

HD = 128
DOCS = (0, 1, -1, 2, -2)
GROUP = 4
STEP = 4
TILE = 8
NEAR = 3
HALVES = 2
VMEM = 64 << 20
FAR = 1e30


def shifted(value, axis, steps):
    count = lax.axis_size(axis)
    pairs = [(source, (source + steps) % count) for source in range(count)]
    return lax.ppermute(value, axis, pairs)


def swapped(value, axis, mask):
    pairs = [(source, source ^ mask) for source in range(lax.axis_size(axis))]
    return lax.ppermute(value, axis, pairs)


def dot_nt(a, b):
    return lax.dot_general(a, b, (((1,), (1,)), ((), ())), preferred_element_type=jnp.float32)


def dot_nn(a, b):
    return lax.dot_general(a, b, (((1,), (0,)), ((), ())), preferred_element_type=jnp.float32)


def scores_of(keys, query_rows, own_first):
    scores = dot_nt(keys, query_rows) * (HD ** (-0.5))
    if not own_first:
        return scores
    rows = keys.shape[0]
    own = scores[:, :rows]
    key_at = lax.broadcasted_iota(jnp.int32, own.shape, 0)
    query_at = lax.broadcasted_iota(jnp.int32, own.shape, 1)
    own = jnp.where(key_at <= query_at, own, -FAR)
    return jnp.concatenate([own, scores[:, rows:]], 1)


def head_rows(refs, head):
    return jnp.concatenate([ref[:, head * HD : (head + 1) * HD] for ref in refs], 0)


def stats_kernel(low, steps, offsets_ref, keys_ref, values_ref, *refs):
    count = (len(refs) - 1) // 2
    query_refs, grad_refs, out_ref = refs[:count], refs[count : 2 * count], refs[-1]
    before_ref = refs[2 * count] if low else None
    rows = keys_ref.shape[0]
    step = pl.program_id(0)
    base = pl.multiple_of(step * TILE, TILE)
    for head in range(STEP):
        cols = slice(head * HD, (head + 1) * HD)
        scores = scores_of(keys_ref[:, cols], head_rows(query_refs, head), low == 0)
        prob_grad = dot_nt(values_ref[:, cols], head_rows(grad_refs, head))
        top = jnp.max(scores, 0, keepdims=True)
        weights = jnp.exp(scores - top)
        total = jnp.sum(weights, 0, keepdims=True)
        mean = jnp.sum(weights * prob_grad, 0, keepdims=True) / total
        lse = top + jnp.log(total)
        for doc in range(count):
            cut = slice(doc * rows, (doc + 1) * rows)
            start = base + (low + doc) * steps * TILE
            out_ref[pl.ds(start + head, 1), :] = lse[:, cut]
            out_ref[pl.ds(start + STEP + head, 1), :] = mean[:, cut]

    @pl.when(step == 0)
    def _():
        if low:
            out_ref[: before_ref.shape[0], :] = before_ref[...]
            tail = out_ref.shape[0] - TILE
            for slot in range(2):
                value = offsets_ref[0, slot].astype(jnp.float32)
                at = tail + slot * STEP
                out_ref[at : at + STEP, :] = jnp.full((STEP, rows), value, jnp.float32)


def merged(stat_ref, me, step, steps):
    stride = stat_ref.shape[0] // (3 * GROUP)

    def tile(place, row):
        return stat_ref[pl.ds(pl.multiple_of(place * stride + row, TILE), TILE), :]

    lse_rows, delta_rows = [], []
    for doc in DOCS:
        owner = me + GROUP + doc
        offsets = tile(owner, stride - TILE)
        first, second = offsets[:STEP], offsets[STEP:]
        parts = []
        for hop in DOCS:
            stat = tile(owner + hop, (DOCS.index(-hop) * steps + step) * TILE)
            lse, mean = stat[:STEP], stat[STEP:]
            if hop:
                lse = jnp.where((first == hop) | (second == hop), lse, -FAR)
            parts.append((lse, mean))
        top = functools.reduce(jnp.maximum, [lse for lse, _ in parts])
        weights = [jnp.exp(lse - top) for lse, _ in parts]
        total = sum(weights)
        delta = sum(weight * mean for weight, (_, mean) in zip(weights, parts)) / total
        lse = top + jnp.log(total)
        if doc:
            lse = jnp.where((first == -doc) | (second == -doc), lse, FAR)
        lse_rows.append(lse)
        delta_rows.append(delta)
    return jnp.concatenate(lse_rows, 1), jnp.concatenate(delta_rows, 1)


def grads_kernel(first_step, steps, place_ref, *refs):
    count = len(DOCS)
    stat_refs, (keys_ref, values_ref), refs = refs[:3], refs[3:5], refs[5:]
    query_refs, grad_refs = refs[:count], refs[count : 2 * count]
    key_half, key_out, value_out, stat_ref = refs[-4:]
    each = stat_refs[0].shape[0]

    @pl.when(pl.program_id(0) == 0)
    def _():
        for at, ref in enumerate(stat_refs):
            stat_ref[at * each : (at + 1) * each, :] = ref[...]

    step = pl.program_id(0) + first_step
    lse, delta = merged(stat_ref, place_ref[0], step, steps)
    for head in range(STEP):
        cols = slice(head * HD, (head + 1) * HD)
        query_rows = head_rows(query_refs, head)
        grad_rows = head_rows(grad_refs, head)
        scores = scores_of(keys_ref[:, cols], query_rows, True)
        prob_grad = dot_nt(values_ref[:, cols], grad_rows)
        probs = jnp.exp(scores - lse[head : head + 1])
        score_grad = probs * (prob_grad - delta[head : head + 1]) * (HD ** (-0.5))
        key_total = dot_nn(score_grad.astype(jnp.bfloat16), query_rows).astype(jnp.bfloat16)
        value_total = dot_nn(probs.astype(jnp.bfloat16), grad_rows)
        key_half[:, cols] = key_total
        key_out[:, cols] = key_total
        value_out[:, cols] = value_total.astype(jnp.bfloat16)


def weight_kernel(inputs_ref, *refs):
    grads = jnp.concatenate([ref[...] for ref in refs[:4]], 0)
    refs[-1][...] = dot_nn(inputs_ref[...], grads).astype(jnp.bfloat16)


def local(layer_input, queries, key_vectors, value_vectors, output_grad, partner_offsets):
    rows, features = queries.shape
    steps = features // (HD * STEP)
    wide = STEP * HD
    docs = len(DOCS)
    mine = lax.axis_index("fsdp")
    places = lax.axis_size("fsdp")
    params = pltpu.CompilerParams(vmem_limit_bytes=VMEM)

    by_doc = {0: (queries, output_grad)}
    up_q, down_q = shifted(queries, "dp", -1), shifted(queries, "dp", 1)
    up_g, down_g = shifted(output_grad, "dp", -1), shifted(output_grad, "dp", 1)
    by_doc[1], by_doc[-1] = (up_q, up_g), (down_q, down_g)
    by_doc[2] = shifted(up_q, "dp", -1), shifted(up_g, "dp", -1)
    by_doc[-2] = shifted(down_q, "dp", 1), shifted(down_g, "dp", 1)
    query_docs = [by_doc[doc][0] for doc in DOCS]
    grad_docs = [by_doc[doc][1] for doc in DOCS]

    width = layer_input.shape[1] // places
    columns = []
    for k in range(places):
        piece = lax.dynamic_slice_in_dim(layer_input, (mine ^ k) * width, width, 1)
        columns.append(swapped(piece, "fsdp", k) if k else piece)
    columns = jnp.concatenate(columns, 0).T
    grad_docs[-1], columns = lax.optimization_barrier((grad_docs[-1], columns))

    block = pl.BlockSpec((rows, wide), lambda step: (0, step))
    pair = rows * rows * HD * 2 * (features // HD)
    exps = rows * rows * (features // HD)
    stats = None
    for low, high in ((0, NEAR), (NEAR, docs)):
        out_rows = high * steps * TILE + (TILE if high == docs else 0)
        before = [] if stats is None else [stats]
        stats = pl.pallas_call(
            functools.partial(stats_kernel, low, steps),
            grid=(steps,),
            in_specs=[pl.BlockSpec(memory_space=pltpu.SMEM)]
            + [block] * (2 + 2 * (high - low))
            + [pl.BlockSpec(array.shape, lambda step: (0, 0)) for array in before],
            out_specs=pl.BlockSpec((out_rows, rows), lambda step: (0, 0)),
            out_shape=jax.ShapeDtypeStruct((out_rows, rows), jnp.float32),
            compiler_params=params,
            cost_estimate=pl.CostEstimate(
                flops=2 * pair * (high - low),
                bytes_accessed=2 * (high - low + 1) * rows * features * 2,
                transcendentals=exps * (high - low),
            ),
            name="stats",
        )(
            partner_offsets,
            key_vectors,
            value_vectors,
            *query_docs[low:high],
            *grad_docs[low:high],
            *before,
        )

    replicas = lax.axis_size("dp")
    groups = [list(range(low, low + GROUP)) for low in range(0, replicas, GROUP)]
    here = lax.all_gather(stats, "dp", axis=0, tiled=True, axis_index_groups=groups)
    stat_parts = [shifted(here, "dp", GROUP), here, shifted(here, "dp", -GROUP)]
    place = (lax.axis_index("dp") % GROUP).astype(jnp.int32).reshape(1)

    each = steps // HALVES
    any_space = pl.BlockSpec(memory_space=pl.ANY)
    full = jax.ShapeDtypeStruct((rows, features), jnp.bfloat16)
    half_shape = jax.ShapeDtypeStruct((rows, each * wide), jnp.bfloat16)
    key_parts, key_grad, value_grad = [], None, None
    for half in range(HALVES):
        low = half * each
        at_half = pl.BlockSpec((rows, wide), lambda step, low=low: (0, step + low))
        inputs = [place, *stat_parts, key_vectors, value_vectors, *query_docs, *grad_docs]
        held = [] if half == 0 else [key_grad, value_grad]
        key_part, key_grad, value_grad = pl.pallas_call(
            functools.partial(grads_kernel, low, steps),
            grid=(each,),
            in_specs=[pl.BlockSpec(memory_space=pltpu.SMEM)]
            + [pl.BlockSpec(here.shape, lambda step: (0, 0))] * 3
            + [at_half] * (2 + 2 * docs)
            + [any_space] * len(held),
            out_specs=[block, at_half, at_half],
            out_shape=[half_shape, full, full],
            scratch_shapes=[pltpu.VMEM((3 * here.shape[0], rows), jnp.float32)],
            input_output_aliases={len(inputs) + at: 1 + at for at in range(len(held))},
            compiler_params=params,
            cost_estimate=pl.CostEstimate(
                flops=4 * pair * docs // HALVES,
                bytes_accessed=15 * rows * features * 2 // HALVES,
                transcendentals=exps * docs // HALVES,
            ),
            name="grads",
        )(*inputs, *held)
        key_parts.append(key_part)

    beside = swapped(key_grad, "fsdp", 1)
    weight = None
    for half in range(HALVES):
        low = half * each
        at_half = pl.BlockSpec((rows, wide), lambda step, low=low: (0, step + low))
        across = swapped(key_parts[half], "fsdp", 2)
        inputs = [columns, key_grad, beside, across, swapped(across, "fsdp", 1)]
        held = [] if weight is None else [weight]
        weight = pl.pallas_call(
            weight_kernel,
            grid=(each,),
            in_specs=[pl.BlockSpec(columns.shape, lambda step: (0, 0)), at_half, at_half, block, block]
            + [any_space] * len(held),
            out_specs=pl.BlockSpec((width, wide), lambda step, low=low: (0, step + low)),
            out_shape=jax.ShapeDtypeStruct((width, features), jnp.bfloat16),
            input_output_aliases={len(inputs): 0} if held else {},
            compiler_params=params,
            cost_estimate=pl.CostEstimate(
                flops=2 * width * columns.shape[1] * each * wide,
                bytes_accessed=2 * each * wide * (columns.shape[1] + width),
                transcendentals=0,
            ),
            name="weight",
        )(*inputs, *held)
    return weight[None], value_grad


def solution(mesh):
    return jax.shard_map(
        local,
        mesh=mesh,
        in_specs=(
            P(("dp", "fsdp"), None),
            P(("dp", "fsdp"), None),
            P(("dp", "fsdp"), None),
            P(("dp", "fsdp"), None),
            P(("dp", "fsdp"), None),
            P("dp", None),
        ),
        out_specs=(P("dp", "fsdp", None), P(("dp", "fsdp"), None)),
        check_vma=False,
    )
```

```python
import functools

import jax
import jax.numpy as jnp
from jax import lax
from jax.experimental import pallas as pl
from jax.experimental.pallas import tpu as pltpu
from jax.sharding import PartitionSpec as P

HD = 128
DOCS = (0, 1, -1, 2, -2)
GROUP = 4
STEP = 4
TILE = 8
NEAR = 3
HALVES = 2
VMEM = 64 << 20
FAR = 1e30


def traded(value, axis, size, odd):
    count = lax.axis_size(axis)
    blocks = count // size
    pairs = []
    for source in range(count):
        block = source // size
        step = 1 if (block % 2 == 1) == odd else -1
        pairs.append((source, (block + step) % blocks * size + source % size))
    return lax.ppermute(value, axis, pairs)


def swapped(value, axis, mask):
    pairs = [(source, source ^ mask) for source in range(lax.axis_size(axis))]
    return lax.ppermute(value, axis, pairs)


def dot_nt(a, b):
    return lax.dot_general(a, b, (((1,), (1,)), ((), ())), preferred_element_type=jnp.float32)


def dot_nn(a, b):
    return lax.dot_general(a, b, (((1,), (0,)), ((), ())), preferred_element_type=jnp.float32)


def scores_of(keys, query_rows, own_first):
    scores = dot_nt(keys, query_rows) * (HD ** (-0.5))
    if not own_first:
        return scores
    rows = keys.shape[0]
    own = scores[:, :rows]
    key_at = lax.broadcasted_iota(jnp.int32, own.shape, 0)
    query_at = lax.broadcasted_iota(jnp.int32, own.shape, 1)
    own = jnp.where(key_at <= query_at, own, -FAR)
    return jnp.concatenate([own, scores[:, rows:]], 1)


def head_rows(refs, head):
    return jnp.concatenate([ref[:, head * HD : (head + 1) * HD] for ref in refs], 0)


def stats_kernel(low, steps, offsets_ref, keys_ref, values_ref, *refs):
    count = (len(refs) - 1) // 2
    query_refs, grad_refs, out_ref = refs[:count], refs[count : 2 * count], refs[-1]
    before_ref = refs[2 * count] if low else None
    rows = keys_ref.shape[0]
    step = pl.program_id(0)
    base = pl.multiple_of(step * TILE, TILE)
    for head in range(STEP):
        cols = slice(head * HD, (head + 1) * HD)
        scores = scores_of(keys_ref[:, cols], head_rows(query_refs, head), low == 0)
        prob_grad = dot_nt(values_ref[:, cols], head_rows(grad_refs, head))
        top = jnp.max(scores, 0, keepdims=True)
        weights = jnp.exp(scores - top)
        total = jnp.sum(weights, 0, keepdims=True)
        mean = jnp.sum(weights * prob_grad, 0, keepdims=True) / total
        lse = top + jnp.log(total)
        for doc in range(count):
            cut = slice(doc * rows, (doc + 1) * rows)
            start = base + (low + doc) * steps * TILE
            out_ref[pl.ds(start + head, 1), :] = lse[:, cut]
            out_ref[pl.ds(start + STEP + head, 1), :] = mean[:, cut]

    if low:
        each = out_ref.shape[0] // GROUP

        @pl.when(step == steps - 1)
        def _():
            out_ref[: before_ref.shape[0], :] = before_ref[...]
            for slot in range(2):
                value = offsets_ref[0, slot].astype(jnp.float32)
                at = each - TILE + slot * STEP
                out_ref[at : at + STEP, :] = jnp.full((STEP, rows), value, jnp.float32)
            for copy in range(1, GROUP):
                out_ref[copy * each : (copy + 1) * each, :] = out_ref[:each, :]


def merged(stat_ref, me, step, steps):
    stride = stat_ref.shape[0] // (3 * GROUP)
    sign = 1 - 2 * (me % 2)
    sign_real = sign.astype(jnp.float32)

    def tile(hops, row):
        place = me + GROUP + sign * hops
        return stat_ref[pl.ds(pl.multiple_of(place * stride + row, TILE), TILE), :]

    lse_rows, delta_rows = [], []
    for doc in DOCS:
        offsets = tile(doc, stride - TILE) * sign_real
        first, second = offsets[:STEP], offsets[STEP:]
        parts = []
        for hop in DOCS:
            name = -hop if (doc + hop) % 2 == 0 else hop
            stat = tile(doc + hop, (DOCS.index(name) * steps + step) * TILE)
            lse, mean = stat[:STEP], stat[STEP:]
            if hop:
                lse = jnp.where((first == hop) | (second == hop), lse, -FAR)
            parts.append((lse, mean))
        top = functools.reduce(jnp.maximum, [lse for lse, _ in parts])
        weights = [jnp.exp(lse - top) for lse, _ in parts]
        total = sum(weights)
        delta = sum(weight * mean for weight, (_, mean) in zip(weights, parts)) / total
        lse = top + jnp.log(total)
        if doc:
            lse = jnp.where((first == -doc) | (second == -doc), lse, FAR)
        lse_rows.append(lse)
        delta_rows.append(delta)
    return jnp.concatenate(lse_rows, 1), jnp.concatenate(delta_rows, 1)


def grads_kernel(first_step, steps, place_ref, *refs):
    count = len(DOCS)
    stat_refs, (keys_ref, values_ref), refs = refs[:3], refs[3:5], refs[5:]
    query_refs, grad_refs = refs[:count], refs[count : 2 * count]
    key_half, key_out, value_out, stat_ref = refs[-4:]
    each = stat_refs[0].shape[0]

    @pl.when(pl.program_id(0) == 0)
    def _():
        above = 2 - 2 * place_ref[1]
        for at, ref in ((above, stat_refs[0]), (1, stat_refs[1]), (2 - above, stat_refs[2])):
            stat_ref[pl.ds(pl.multiple_of(at * each, TILE), each), :] = ref[...]

    step = pl.program_id(0) + first_step
    lse, delta = merged(stat_ref, place_ref[0], step, steps)
    for head in range(STEP):
        cols = slice(head * HD, (head + 1) * HD)
        query_rows = head_rows(query_refs, head)
        grad_rows = head_rows(grad_refs, head)
        scores = scores_of(keys_ref[:, cols], query_rows, True)
        prob_grad = dot_nt(values_ref[:, cols], grad_rows)
        probs = jnp.exp(scores - lse[head : head + 1])
        score_grad = probs * (prob_grad - delta[head : head + 1]) * (HD ** (-0.5))
        key_total = dot_nn(score_grad.astype(jnp.bfloat16), query_rows).astype(jnp.bfloat16)
        value_total = dot_nn(probs.astype(jnp.bfloat16), grad_rows)
        key_half[:, cols] = key_total
        key_out[:, cols] = key_total
        value_out[:, cols] = value_total.astype(jnp.bfloat16)


def weight_kernel(inputs_ref, *refs):
    grads = jnp.concatenate([ref[...] for ref in refs[:4]], 0)
    refs[-1][...] = dot_nn(inputs_ref[...], grads).astype(jnp.bfloat16)


def local(layer_input, queries, key_vectors, value_vectors, output_grad, partner_offsets):
    rows, features = queries.shape
    steps = features // (HD * STEP)
    wide = STEP * HD
    docs = len(DOCS)
    mine = lax.axis_index("fsdp")
    places = lax.axis_size("fsdp")
    params = pltpu.CompilerParams(vmem_limit_bytes=VMEM)

    others = [traded(array, "dp", 1, True) for array in (queries, output_grad)]
    firsts = [traded(array, "dp", 1, False) for array in (queries, output_grad)]
    near = list(zip(firsts, others))
    seconds = [traded(first, "dp", 1, True) for first in firsts]
    far = list(zip([traded(other, "dp", 1, False) for other in others], seconds))
    query_docs, grad_docs = (
        [array, *near[at], *far[at]] for at, array in enumerate((queries, output_grad))
    )

    width = layer_input.shape[1] // places
    columns = []
    for k in range(places):
        piece = lax.dynamic_slice_in_dim(layer_input, (mine ^ k) * width, width, 1)
        columns.append(swapped(piece, "fsdp", k) if k else piece)
    columns = jnp.concatenate(columns, 0).T
    grad_docs[-1], columns = lax.optimization_barrier((grad_docs[-1], columns))

    block = pl.BlockSpec((rows, wide), lambda step: (0, step))
    pair = rows * rows * HD * 2 * (features // HD)
    exps = rows * rows * (features // HD)
    stats = None
    for low, high in ((0, NEAR), (NEAR, docs)):
        out_rows = high * steps * TILE if high < docs else GROUP * (docs * steps + 1) * TILE
        before = [] if stats is None else [stats]
        stats = pl.pallas_call(
            functools.partial(stats_kernel, low, steps),
            grid=(steps,),
            in_specs=[pl.BlockSpec(memory_space=pltpu.SMEM)]
            + [block] * (2 + 2 * (high - low))
            + [pl.BlockSpec(array.shape, lambda step: (0, 0)) for array in before],
            out_specs=pl.BlockSpec((out_rows, rows), lambda step: (0, 0)),
            out_shape=jax.ShapeDtypeStruct((out_rows, rows), jnp.float32),
            compiler_params=params,
            cost_estimate=pl.CostEstimate(
                flops=2 * pair * (high - low),
                bytes_accessed=2 * (high - low + 1) * rows * features * 2,
                transcendentals=exps * (high - low),
            ),
            name="stats",
        )(
            partner_offsets,
            key_vectors,
            value_vectors,
            *query_docs[low:high],
            *grad_docs[low:high],
            *before,
        )

    replicas = lax.axis_size("dp")
    groups = [list(range(low, low + GROUP)) for low in range(0, replicas, GROUP)]
    here = lax.all_to_all(stats, "dp", 0, 0, axis_index_groups=groups, tiled=True)
    after_odd = traded(here, "dp", GROUP, True)
    stat_parts = [traded(here, "dp", GROUP, False), here, after_odd]
    replica = lax.axis_index("dp")
    place = jnp.stack([replica % GROUP, replica // GROUP % 2]).astype(jnp.int32)

    each = steps // HALVES
    any_space = pl.BlockSpec(memory_space=pl.ANY)
    full = jax.ShapeDtypeStruct((rows, features), jnp.bfloat16)
    half_shape = jax.ShapeDtypeStruct((rows, each * wide), jnp.bfloat16)
    key_parts, key_grad, value_grad = [], None, None
    for half in range(HALVES):
        low = half * each
        at_half = pl.BlockSpec((rows, wide), lambda step, low=low: (0, step + low))
        inputs = [place, *stat_parts, key_vectors, value_vectors, *query_docs, *grad_docs]
        held = [] if half == 0 else [key_grad, value_grad]
        key_part, key_grad, value_grad = pl.pallas_call(
            functools.partial(grads_kernel, low, steps),
            grid=(each,),
            in_specs=[pl.BlockSpec(memory_space=pltpu.SMEM)]
            + [pl.BlockSpec(here.shape, lambda step: (0, 0))] * 3
            + [at_half] * (2 + 2 * docs)
            + [any_space] * len(held),
            out_specs=[block, at_half, at_half],
            out_shape=[half_shape, full, full],
            scratch_shapes=[pltpu.VMEM((3 * here.shape[0], rows), jnp.float32)],
            input_output_aliases={len(inputs) + at: 1 + at for at in range(len(held))},
            compiler_params=params,
            cost_estimate=pl.CostEstimate(
                flops=4 * pair * docs // HALVES,
                bytes_accessed=15 * rows * features * 2 // HALVES,
                transcendentals=exps * docs // HALVES,
            ),
            name="grads",
        )(*inputs, *held)
        key_parts.append(key_part)

    beside = swapped(key_grad, "fsdp", 1)
    weight = None
    for half in range(HALVES):
        low = half * each
        at_half = pl.BlockSpec((rows, wide), lambda step, low=low: (0, step + low))
        across = swapped(key_parts[half], "fsdp", 2)
        inputs = [columns, key_grad, beside, across, swapped(across, "fsdp", 1)]
        held = [] if weight is None else [weight]
        weight = pl.pallas_call(
            weight_kernel,
            grid=(each,),
            in_specs=[pl.BlockSpec(columns.shape, lambda step: (0, 0)), at_half, at_half, block, block]
            + [any_space] * len(held),
            out_specs=pl.BlockSpec((width, wide), lambda step, low=low: (0, step + low)),
            out_shape=jax.ShapeDtypeStruct((width, features), jnp.bfloat16),
            input_output_aliases={len(inputs): 0} if held else {},
            compiler_params=params,
            cost_estimate=pl.CostEstimate(
                flops=2 * width * columns.shape[1] * each * wide,
                bytes_accessed=2 * each * wide * (columns.shape[1] + width),
                transcendentals=0,
            ),
            name="weight",
        )(*inputs, *held)
    return weight[None], value_grad


def solution(mesh):
    return jax.shard_map(
        local,
        mesh=mesh,
        in_specs=(
            P(("dp", "fsdp"), None),
            P(("dp", "fsdp"), None),
            P(("dp", "fsdp"), None),
            P(("dp", "fsdp"), None),
            P(("dp", "fsdp"), None),
            P("dp", None),
        ),
        out_specs=(P("dp", "fsdp", None), P(("dp", "fsdp"), None)),
        check_vma=False,
    )
```

```python
import functools

import jax
import jax.numpy as jnp
from jax import lax
from jax.experimental import pallas as pl
from jax.experimental.pallas import tpu as pltpu
from jax.sharding import PartitionSpec as P

HD = 128
DOCS = (0, 1, -1, 2, -2)
GROUP = 4
STEP = 4
TILE = 8
NEAR = 3
HALVES = 2
VMEM = 64 << 20
FAR = 1e30


def traded(value, axis, size, odd):
    count = lax.axis_size(axis)
    blocks = count // size
    pairs = []
    for source in range(count):
        block = source // size
        step = 1 if (block % 2 == 1) == odd else -1
        pairs.append((source, (block + step) % blocks * size + source % size))
    return lax.ppermute(value, axis, pairs)


def swapped(value, axis, mask):
    pairs = [(source, source ^ mask) for source in range(lax.axis_size(axis))]
    return lax.ppermute(value, axis, pairs)


def dot_nt(a, b):
    return lax.dot_general(a, b, (((1,), (1,)), ((), ())), preferred_element_type=jnp.float32)


def dot_nn(a, b):
    return lax.dot_general(a, b, (((1,), (0,)), ((), ())), preferred_element_type=jnp.float32)


def scores_of(keys, query_rows, own_first):
    scores = dot_nt(keys, query_rows) * (HD ** (-0.5))
    if not own_first:
        return scores
    rows = keys.shape[0]
    own = scores[:, :rows]
    key_at = lax.broadcasted_iota(jnp.int32, own.shape, 0)
    query_at = lax.broadcasted_iota(jnp.int32, own.shape, 1)
    own = jnp.where(key_at <= query_at, own, -FAR)
    return jnp.concatenate([own, scores[:, rows:]], 1)


def head_rows(refs, head):
    return jnp.concatenate([ref[:, head * HD : (head + 1) * HD] for ref in refs], 0)


def stats_kernel(low, steps, offsets_ref, keys_ref, values_ref, *refs):
    count = (len(refs) - 1) // 2
    query_refs, grad_refs, out_ref = refs[:count], refs[count : 2 * count], refs[-1]
    before_ref = refs[2 * count] if low else None
    rows = keys_ref.shape[0]
    step = pl.program_id(0)
    base = pl.multiple_of(step * TILE, TILE)
    for head in range(STEP):
        cols = slice(head * HD, (head + 1) * HD)
        scores = scores_of(keys_ref[:, cols], head_rows(query_refs, head), low == 0)
        prob_grad = dot_nt(values_ref[:, cols], head_rows(grad_refs, head))
        top = jnp.max(scores, 0, keepdims=True)
        weights = jnp.exp(scores - top)
        total = jnp.sum(weights, 0, keepdims=True)
        mean = jnp.sum(weights * prob_grad, 0, keepdims=True) / total
        lse = top + jnp.log(total)
        for doc in range(count):
            cut = slice(doc * rows, (doc + 1) * rows)
            start = base + (low + doc) * steps * TILE
            out_ref[pl.ds(start + head, 1), :] = lse[:, cut]
            out_ref[pl.ds(start + STEP + head, 1), :] = mean[:, cut]

    if low:
        each = out_ref.shape[0] // GROUP

        @pl.when(step == steps - 1)
        def _():
            out_ref[: before_ref.shape[0], :] = before_ref[...]
            for slot in range(2):
                value = offsets_ref[0, slot].astype(jnp.float32)
                at = each - TILE + slot * STEP
                out_ref[at : at + STEP, :] = jnp.full((STEP, rows), value, jnp.float32)
            for copy in range(1, GROUP):
                out_ref[copy * each : (copy + 1) * each, :] = out_ref[:each, :]


def merged(stat_ref, me, step, steps):
    stride = stat_ref.shape[0] // (3 * GROUP)
    sign = 1 - 2 * (me % 2)
    sign_real = sign.astype(jnp.float32)

    def tile(hops, row):
        place = me + GROUP + sign * hops
        return stat_ref[pl.ds(pl.multiple_of(place * stride + row, TILE), TILE), :]

    lse_rows, delta_rows = [], []
    for doc in DOCS:
        offsets = tile(doc, stride - TILE) * sign_real
        first, second = offsets[:STEP], offsets[STEP:]
        parts = []
        for hop in DOCS:
            name = -hop if (doc + hop) % 2 == 0 else hop
            stat = tile(doc + hop, (DOCS.index(name) * steps + step) * TILE)
            lse, mean = stat[:STEP], stat[STEP:]
            if hop:
                lse = jnp.where((first == hop) | (second == hop), lse, -FAR)
            parts.append((lse, mean))
        top = functools.reduce(jnp.maximum, [lse for lse, _ in parts])
        weights = [jnp.exp(lse - top) for lse, _ in parts]
        total = sum(weights)
        delta = sum(weight * mean for weight, (_, mean) in zip(weights, parts)) / total
        lse = top + jnp.log(total)
        if doc:
            lse = jnp.where((first == -doc) | (second == -doc), lse, FAR)
        lse_rows.append(lse)
        delta_rows.append(delta)
    return jnp.concatenate(lse_rows, 1), jnp.concatenate(delta_rows, 1)


def grads_kernel(first_step, steps, place_ref, *refs):
    count = len(DOCS)
    stat_refs, (keys_ref, values_ref), refs = refs[:3], refs[3:5], refs[5:]
    query_refs, grad_refs = refs[:count], refs[count : 2 * count]
    key_half, key_out, value_out, stat_ref = refs[-4:]
    each = stat_refs[0].shape[0]

    @pl.when(pl.program_id(0) == 0)
    def _():
        above = 2 - 2 * place_ref[1]
        for at, ref in ((above, stat_refs[0]), (1, stat_refs[1]), (2 - above, stat_refs[2])):
            stat_ref[pl.ds(pl.multiple_of(at * each, TILE), each), :] = ref[...]

    step = pl.program_id(0) + first_step
    lse, delta = merged(stat_ref, place_ref[0], step, steps)
    for head in range(STEP):
        cols = slice(head * HD, (head + 1) * HD)
        query_rows = head_rows(query_refs, head)
        grad_rows = head_rows(grad_refs, head)
        scores = scores_of(keys_ref[:, cols], query_rows, True)
        prob_grad = dot_nt(values_ref[:, cols], grad_rows)
        probs = jnp.exp(scores - lse[head : head + 1])
        score_grad = probs * (prob_grad - delta[head : head + 1]) * (HD ** (-0.5))
        key_total = dot_nn(score_grad.astype(jnp.bfloat16), query_rows).astype(jnp.bfloat16)
        value_total = dot_nn(probs.astype(jnp.bfloat16), grad_rows)
        key_half[:, cols] = key_total
        key_out[:, cols] = key_total
        value_out[:, cols] = value_total.astype(jnp.bfloat16)


def weight_kernel(inputs_ref, *refs):
    grads = jnp.concatenate([ref[...] for ref in refs[:4]], 0)
    refs[-1][...] = dot_nn(inputs_ref[...], grads).astype(jnp.bfloat16)


def local(layer_input, queries, key_vectors, value_vectors, output_grad, partner_offsets):
    rows, features = queries.shape
    steps = features // (HD * STEP)
    wide = STEP * HD
    docs = len(DOCS)
    mine = lax.axis_index("fsdp")
    places = lax.axis_size("fsdp")
    params = pltpu.CompilerParams(vmem_limit_bytes=VMEM)

    others = [traded(array, "dp", 1, True) for array in (queries, output_grad)]
    firsts = [traded(array, "dp", 1, False) for array in (queries, output_grad)]
    near = list(zip(firsts, others))
    seconds = [traded(first, "dp", 1, True) for first in firsts]
    far = list(zip([traded(other, "dp", 1, False) for other in others], seconds))
    query_docs, grad_docs = (
        [array, *near[at], *far[at]] for at, array in enumerate((queries, output_grad))
    )

    block = pl.BlockSpec((rows, wide), lambda step: (0, step))
    pair = rows * rows * HD * 2 * (features // HD)
    exps = rows * rows * (features // HD)
    stats = None
    for low, high in ((0, NEAR), (NEAR, docs)):
        out_rows = high * steps * TILE if high < docs else GROUP * (docs * steps + 1) * TILE
        before = [] if stats is None else [stats]
        stats = pl.pallas_call(
            functools.partial(stats_kernel, low, steps),
            grid=(steps,),
            in_specs=[pl.BlockSpec(memory_space=pltpu.SMEM)]
            + [block] * (2 + 2 * (high - low))
            + [pl.BlockSpec(array.shape, lambda step: (0, 0)) for array in before],
            out_specs=pl.BlockSpec((out_rows, rows), lambda step: (0, 0)),
            out_shape=jax.ShapeDtypeStruct((out_rows, rows), jnp.float32),
            compiler_params=params,
            cost_estimate=pl.CostEstimate(
                flops=2 * pair * (high - low),
                bytes_accessed=2 * (high - low + 1) * rows * features * 2,
                transcendentals=exps * (high - low),
            ),
            name="stats",
        )(
            partner_offsets,
            key_vectors,
            value_vectors,
            *query_docs[low:high],
            *grad_docs[low:high],
            *before,
        )

    replicas = lax.axis_size("dp")
    groups = [list(range(low, low + GROUP)) for low in range(0, replicas, GROUP)]
    here = lax.all_to_all(stats, "dp", 0, 0, axis_index_groups=groups, tiled=True)
    width = layer_input.shape[1] // places
    here, layer_input = lax.optimization_barrier((here, layer_input))
    columns = []
    for k in range(places):
        piece = lax.dynamic_slice_in_dim(layer_input, (mine ^ k) * width, width, 1)
        columns.append(swapped(piece, "fsdp", k) if k else piece)
    columns = jnp.concatenate(columns, 0).T

    after_odd = traded(here, "dp", GROUP, True)
    stat_parts = [traded(here, "dp", GROUP, False), here, after_odd]
    stat_parts[2], columns = lax.optimization_barrier((stat_parts[2], columns))
    replica = lax.axis_index("dp")
    place = jnp.stack([replica % GROUP, replica // GROUP % 2]).astype(jnp.int32)

    each = steps // HALVES
    any_space = pl.BlockSpec(memory_space=pl.ANY)
    full = jax.ShapeDtypeStruct((rows, features), jnp.bfloat16)
    half_shape = jax.ShapeDtypeStruct((rows, each * wide), jnp.bfloat16)
    key_parts, key_grad, value_grad = [], None, None
    for half in range(HALVES):
        low = half * each
        at_half = pl.BlockSpec((rows, wide), lambda step, low=low: (0, step + low))
        inputs = [place, *stat_parts, key_vectors, value_vectors, *query_docs, *grad_docs]
        held = [] if half == 0 else [key_grad, value_grad]
        key_part, key_grad, value_grad = pl.pallas_call(
            functools.partial(grads_kernel, low, steps),
            grid=(each,),
            in_specs=[pl.BlockSpec(memory_space=pltpu.SMEM)]
            + [pl.BlockSpec(here.shape, lambda step: (0, 0))] * 3
            + [at_half] * (2 + 2 * docs)
            + [any_space] * len(held),
            out_specs=[block, at_half, at_half],
            out_shape=[half_shape, full, full],
            scratch_shapes=[pltpu.VMEM((3 * here.shape[0], rows), jnp.float32)],
            input_output_aliases={len(inputs) + at: 1 + at for at in range(len(held))},
            compiler_params=params,
            cost_estimate=pl.CostEstimate(
                flops=4 * pair * docs // HALVES,
                bytes_accessed=15 * rows * features * 2 // HALVES,
                transcendentals=exps * docs // HALVES,
            ),
            name="grads",
        )(*inputs, *held)
        key_parts.append(key_part)

    beside = swapped(key_grad, "fsdp", 1)
    weight = None
    for half in range(HALVES):
        low = half * each
        at_half = pl.BlockSpec((rows, wide), lambda step, low=low: (0, step + low))
        across = swapped(key_parts[half], "fsdp", 2)
        inputs = [columns, key_grad, beside, across, swapped(across, "fsdp", 1)]
        held = [] if weight is None else [weight]
        weight = pl.pallas_call(
            weight_kernel,
            grid=(each,),
            in_specs=[pl.BlockSpec(columns.shape, lambda step: (0, 0)), at_half, at_half, block, block]
            + [any_space] * len(held),
            out_specs=pl.BlockSpec((width, wide), lambda step, low=low: (0, step + low)),
            out_shape=jax.ShapeDtypeStruct((width, features), jnp.bfloat16),
            input_output_aliases={len(inputs): 0} if held else {},
            compiler_params=params,
            cost_estimate=pl.CostEstimate(
                flops=2 * width * columns.shape[1] * each * wide,
                bytes_accessed=2 * each * wide * (columns.shape[1] + width),
                transcendentals=0,
            ),
            name="weight",
        )(*inputs, *held)
    return weight[None], value_grad


def solution(mesh):
    return jax.shard_map(
        local,
        mesh=mesh,
        in_specs=(
            P(("dp", "fsdp"), None),
            P(("dp", "fsdp"), None),
            P(("dp", "fsdp"), None),
            P(("dp", "fsdp"), None),
            P(("dp", "fsdp"), None),
            P("dp", None),
        ),
        out_specs=(P("dp", "fsdp", None), P(("dp", "fsdp"), None)),
        check_vma=False,
    )
```

```python
import functools

import jax
import jax.numpy as jnp
from jax import lax
from jax.experimental import pallas as pl
from jax.experimental.pallas import tpu as pltpu
from jax.sharding import PartitionSpec as P

HD = 128
DOCS = (0, 1, -1, 2, -2)
GROUP = 4
STEP = 4
TILE = 8
NEAR = 3
HALVES = 2
WIDE = 512
VMEM = pl.BlockSpec(memory_space=pltpu.VMEM)
PARAMS = pltpu.CompilerParams(vmem_limit_bytes=24 << 20)
FAR = 1e30


def traded(value, axis, size, odd):
    count = lax.axis_size(axis)
    blocks = count // size
    pairs = []
    for source in range(count):
        block = source // size
        step = 1 if (block % 2 == 1) == odd else -1
        pairs.append((source, (block + step) % blocks * size + source % size))
    return lax.ppermute(value, axis, pairs)


def swapped(value, axis, mask):
    pairs = [(source, source ^ mask) for source in range(lax.axis_size(axis))]
    return lax.ppermute(value, axis, pairs)


def dot_nt(a, b):
    return lax.dot_general(a, b, (((1,), (1,)), ((), ())), preferred_element_type=jnp.float32)


def dot_nn(a, b):
    return lax.dot_general(a, b, (((1,), (0,)), ((), ())), preferred_element_type=jnp.float32)


def scores_of(keys, query_rows, own_first):
    scores = dot_nt(keys, query_rows) * (HD ** (-0.5))
    if not own_first:
        return scores
    rows = keys.shape[0]
    own = scores[:, :rows]
    key_at = lax.broadcasted_iota(jnp.int32, own.shape, 0)
    query_at = lax.broadcasted_iota(jnp.int32, own.shape, 1)
    own = jnp.where(key_at <= query_at, own, -FAR)
    return jnp.concatenate([own, scores[:, rows:]], 1)


def in_vmem(array):
    return pltpu.with_memory_space_constraint(array, pltpu.VMEM)


def head_rows(refs, cols):
    return jnp.concatenate([ref[:, cols] for ref in refs], 0)


def stats_kernel(low, offsets_ref, keys_ref, values_ref, *refs):
    count = (len(refs) - 1) // 2
    query_refs, grad_refs, out_ref = refs[:count], refs[count : 2 * count], refs[-1]
    rows, features = keys_ref.shape
    steps = features // (STEP * HD)

    def group(step, carry):
        base = pl.multiple_of(step * TILE, TILE)
        for head in range(STEP):
            cols = pl.ds(pl.multiple_of((step * STEP + head) * HD, HD), HD)
            scores = scores_of(keys_ref[:, cols], head_rows(query_refs, cols), low == 0)
            prob_grad = dot_nt(values_ref[:, cols], head_rows(grad_refs, cols))
            top = jnp.max(scores, 0, keepdims=True)
            weights = jnp.exp(scores - top)
            total = jnp.sum(weights, 0, keepdims=True)
            mean = jnp.sum(weights * prob_grad, 0, keepdims=True) / total
            lse = top + jnp.log(total)
            for doc in range(count):
                cut = slice(doc * rows, (doc + 1) * rows)
                start = base + (low + doc) * steps * TILE
                out_ref[pl.ds(start + head, 1), :] = lse[:, cut]
                out_ref[pl.ds(start + STEP + head, 1), :] = mean[:, cut]
        return carry

    lax.fori_loop(0, steps, group, 0)
    if low:
        before_ref = refs[2 * count]
        each = out_ref.shape[0] // GROUP
        out_ref[: before_ref.shape[0], :] = before_ref[...]
        for slot in range(2):
            value = offsets_ref[0, slot].astype(jnp.float32)
            at = each - TILE + slot * STEP
            out_ref[at : at + STEP, :] = jnp.full((STEP, rows), value, jnp.float32)
        for copy in range(1, GROUP):
            out_ref[copy * each : (copy + 1) * each, :] = out_ref[:each, :]


def merged(stat_ref, me, step, steps):
    stride = stat_ref.shape[0] // (3 * GROUP)
    sign = 1 - 2 * (me % 2)
    sign_real = sign.astype(jnp.float32)

    def tile(hops, row):
        place = me + GROUP + sign * hops
        return stat_ref[pl.ds(pl.multiple_of(place * stride + row, TILE), TILE), :]

    lse_rows, delta_rows = [], []
    for doc in DOCS:
        offsets = tile(doc, stride - TILE) * sign_real
        first, second = offsets[:STEP], offsets[STEP:]
        parts = []
        for hop in DOCS:
            name = -hop if (doc + hop) % 2 == 0 else hop
            stat = tile(doc + hop, (DOCS.index(name) * steps + step) * TILE)
            lse, mean = stat[:STEP], stat[STEP:]
            if hop:
                lse = jnp.where((first == hop) | (second == hop), lse, -FAR)
            parts.append((lse, mean))
        top = functools.reduce(jnp.maximum, [lse for lse, _ in parts])
        weights = [jnp.exp(lse - top) for lse, _ in parts]
        total = sum(weights)
        delta = sum(weight * mean for weight, (_, mean) in zip(weights, parts)) / total
        lse = top + jnp.log(total)
        if doc:
            lse = jnp.where((first == -doc) | (second == -doc), lse, FAR)
        lse_rows.append(lse)
        delta_rows.append(delta)
    return jnp.concatenate(lse_rows, 1), jnp.concatenate(delta_rows, 1)


def grads_kernel(first_step, each, place_ref, *refs):
    count = len(DOCS)
    stat_refs, (keys_ref, values_ref), refs = refs[:3], refs[3:5], refs[5:]
    query_refs, grad_refs = refs[:count], refs[count : 2 * count]
    key_out, value_out, stat_ref = refs[-3:]
    steps = keys_ref.shape[1] // (STEP * HD)
    size = stat_refs[0].shape[0]

    above = 2 - 2 * place_ref[1]
    for at, ref in ((above, stat_refs[0]), (1, stat_refs[1]), (2 - above, stat_refs[2])):
        stat_ref[pl.ds(pl.multiple_of(at * size, TILE), size), :] = ref[...]

    def group(at, carry):
        step = at + first_step
        lse, delta = merged(stat_ref, place_ref[0], step, steps)
        for head in range(STEP):
            cols = pl.ds(pl.multiple_of((step * STEP + head) * HD, HD), HD)
            out_cols = pl.ds(pl.multiple_of((at * STEP + head) * HD, HD), HD)
            query_rows = head_rows(query_refs, cols)
            grad_rows = head_rows(grad_refs, cols)
            scores = scores_of(keys_ref[:, cols], query_rows, True)
            prob_grad = dot_nt(values_ref[:, cols], grad_rows)
            probs = jnp.exp(scores - lse[head : head + 1])
            score_grad = probs * (prob_grad - delta[head : head + 1]) * (HD ** (-0.5))
            key_total = dot_nn(score_grad.astype(jnp.bfloat16), query_rows)
            value_total = dot_nn(probs.astype(jnp.bfloat16), grad_rows)
            key_out[:, out_cols] = key_total.astype(jnp.bfloat16)
            value_out[:, out_cols] = value_total.astype(jnp.bfloat16)
        return carry

    lax.fori_loop(0, each, group, 0)


def weight_kernel(inputs_ref, *refs):
    low = pl.multiple_of(pl.program_id(0) * refs[-1].shape[1], HD)
    cols = pl.ds(low, refs[-1].shape[1])
    grads = jnp.concatenate([ref[:, cols] for ref in refs[:4]], 0)
    refs[-1][...] = dot_nn(inputs_ref[...], grads).astype(jnp.bfloat16)


def call_stats(low, high, partner_offsets, arrays, before):
    rows, features = arrays[0].shape
    heads = features // HD
    docs = len(DOCS)
    out_rows = high * heads // STEP * TILE if high < docs else GROUP * (docs * heads // STEP + 1) * TILE
    pairs = rows * rows * heads * (high - low)
    return pl.pallas_call(
        functools.partial(stats_kernel, low),
        in_specs=[pl.BlockSpec(memory_space=pltpu.SMEM)] + [VMEM] * (len(arrays) + len(before)),
        out_specs=VMEM,
        out_shape=pltpu.VMEM((out_rows, rows), jnp.float32),
        compiler_params=PARAMS,
        cost_estimate=pl.CostEstimate(
            flops=4 * pairs * HD, bytes_accessed=2 * len(arrays) * rows * features, transcendentals=pairs
        ),
        name="stats",
    )(partner_offsets, *map(in_vmem, arrays), *map(in_vmem, before))


def call_grads(low, each, place, stat_parts, arrays):
    rows, features = arrays[0].shape
    pairs = rows * rows * len(DOCS) * each * STEP
    half = (rows, each * STEP * HD)
    return pl.pallas_call(
        functools.partial(grads_kernel, low, each),
        in_specs=[pl.BlockSpec(memory_space=pltpu.SMEM)] + [VMEM] * (3 + len(arrays)),
        out_specs=[VMEM, VMEM],
        out_shape=[pltpu.VMEM(half, jnp.bfloat16), pltpu.VMEM(half, jnp.bfloat16)],
        scratch_shapes=[pltpu.VMEM((3 * stat_parts[0].shape[0], rows), jnp.float32)],
        compiler_params=PARAMS,
        cost_estimate=pl.CostEstimate(
            flops=8 * pairs * HD, bytes_accessed=2 * len(arrays) * half[0] * half[1], transcendentals=pairs
        ),
        name="grads",
    )(place, *map(in_vmem, stat_parts), *map(in_vmem, arrays))


def call_weight(low, columns, pieces, features, held):
    half = pieces[0].shape[1]
    blocks = half // WIDE
    width, tokens = columns.shape
    return pl.pallas_call(
        weight_kernel,
        grid=(blocks,),
        in_specs=[VMEM] * (1 + len(pieces)) + [pl.BlockSpec(memory_space=pl.ANY)] * len(held),
        out_specs=pl.BlockSpec((width, WIDE), lambda step: (0, step + low * blocks)),
        out_shape=jax.ShapeDtypeStruct((width, features), jnp.bfloat16),
        input_output_aliases={1 + len(pieces): 0} if held else {},
        compiler_params=PARAMS,
        cost_estimate=pl.CostEstimate(
            flops=2 * width * tokens * half, bytes_accessed=2 * half * (tokens + width), transcendentals=0
        ),
        name="weight",
    )(*map(in_vmem, [columns, *pieces]), *held)


def local(layer_input, queries, key_vectors, value_vectors, output_grad, partner_offsets):
    rows, features = queries.shape
    steps = features // (HD * STEP)
    docs = len(DOCS)
    mine = lax.axis_index("fsdp")
    places = lax.axis_size("fsdp")

    others = [traded(array, "dp", 1, True) for array in (queries, output_grad)]
    firsts = [traded(array, "dp", 1, False) for array in (queries, output_grad)]
    near = list(zip(firsts, others))
    seconds = [traded(first, "dp", 1, True) for first in firsts]
    far = list(zip([traded(other, "dp", 1, False) for other in others], seconds))
    query_docs, grad_docs = (
        [array, *near[at], *far[at]] for at, array in enumerate((queries, output_grad))
    )

    own = [key_vectors, value_vectors]
    stats = call_stats(0, NEAR, partner_offsets, own + query_docs[:NEAR] + grad_docs[:NEAR], [])

    stats = call_stats(NEAR, docs, partner_offsets, own + query_docs[NEAR:] + grad_docs[NEAR:], [stats])

    width = layer_input.shape[1] // places
    stats, layer_input = lax.optimization_barrier((stats, layer_input))
    columns = []
    for k in range(places):
        piece = lax.dynamic_slice_in_dim(layer_input, (mine ^ k) * width, width, 1)
        columns.append(swapped(piece, "fsdp", k) if k else piece)
    columns = jnp.concatenate(columns, 0).T

    replicas = lax.axis_size("dp")
    groups = [list(range(low, low + GROUP)) for low in range(0, replicas, GROUP)]
    here = lax.all_to_all(stats, "dp", 0, 0, axis_index_groups=groups, tiled=True)
    here, columns = lax.optimization_barrier((here, columns))
    after_odd = traded(here, "dp", GROUP, True)
    stat_parts = [traded(here, "dp", GROUP, False), here, after_odd]
    replica = lax.axis_index("dp")
    place = jnp.stack([replica % GROUP, replica // GROUP % 2]).astype(jnp.int32)

    each = steps // HALVES
    arrays = own + query_docs + grad_docs
    parts = [call_grads(half * each, each, place, stat_parts, arrays) for half in range(HALVES)]

    weight = None
    for half, (key_part, _) in enumerate(parts):
        across = swapped(key_part, "fsdp", 2)
        pieces = [key_part, swapped(key_part, "fsdp", 1), across, swapped(across, "fsdp", 1)]
        held = [] if weight is None else [weight]
        weight = call_weight(half, columns, pieces, features, held)
    return weight[None], jnp.concatenate([value_part for _, value_part in parts], 1)


def solution(mesh):
    return jax.shard_map(
        local,
        mesh=mesh,
        in_specs=(
            P(("dp", "fsdp"), None),
            P(("dp", "fsdp"), None),
            P(("dp", "fsdp"), None),
            P(("dp", "fsdp"), None),
            P(("dp", "fsdp"), None),
            P("dp", None),
        ),
        out_specs=(P("dp", "fsdp", None), P(("dp", "fsdp"), None)),
        check_vma=False,
    )
```

```python
import functools

import jax
import jax.numpy as jnp
from jax import lax
from jax.experimental import pallas as pl
from jax.experimental.pallas import tpu as pltpu
from jax.sharding import PartitionSpec as P

HD = 128
DOCS = (0, 1, -1, 2, -2)
GROUP = 4
STEP = 4
TILE = 8
NEAR = 3
HALVES = 2
WIDE = 512
VMEM = pl.BlockSpec(memory_space=pltpu.VMEM)
ANY = pl.BlockSpec(memory_space=pl.ANY)
PARAMS = pltpu.CompilerParams(vmem_limit_bytes=64 << 20)
FAR = 1e30


def traded(value, axis, size, odd):
    count = lax.axis_size(axis)
    blocks = count // size
    pairs = []
    for source in range(count):
        block = source // size
        step = 1 if (block % 2 == 1) == odd else -1
        pairs.append((source, (block + step) % blocks * size + source % size))
    return lax.ppermute(value, axis, pairs)


def swapped(value, axis, mask):
    pairs = [(source, source ^ mask) for source in range(lax.axis_size(axis))]
    return lax.ppermute(value, axis, pairs)


def dot_nt(a, b):
    return lax.dot_general(a, b, (((1,), (1,)), ((), ())), preferred_element_type=jnp.float32)


def dot_nn(a, b):
    return lax.dot_general(a, b, (((1,), (0,)), ((), ())), preferred_element_type=jnp.float32)


def scores_of(keys, query_rows, own_first):
    scores = dot_nt(keys, query_rows) * (HD ** (-0.5))
    if not own_first:
        return scores
    rows = keys.shape[0]
    own = scores[:, :rows]
    key_at = lax.broadcasted_iota(jnp.int32, own.shape, 0)
    query_at = lax.broadcasted_iota(jnp.int32, own.shape, 1)
    own = jnp.where(key_at <= query_at, own, -FAR)
    return jnp.concatenate([own, scores[:, rows:]], 1)


def in_vmem(array):
    return pltpu.with_memory_space_constraint(array, pltpu.VMEM)


def head_rows(refs, cols):
    return jnp.concatenate([ref[:, cols] for ref in refs], 0)


def fetches(refs, buffer, sems, first, step):
    cols = pl.ds(pl.multiple_of((first + step) * STEP * HD, HD), STEP * HD)
    to = pl.ds(pl.multiple_of(step * STEP * HD, HD), STEP * HD)
    return [
        pltpu.make_async_copy(ref.at[:, cols], buffer.at[at, :, to], sems.at[step])
        for at, ref in enumerate(refs)
    ]


def stats_kernel(low, offsets_ref, *refs):
    *refs, out_ref, buffer, sems = refs
    arrays, before = (refs[:-1], refs[-1]) if low else (refs, None)
    count = (len(arrays) - 2) // 2
    rows, features = arrays[0].shape
    steps = features // (STEP * HD)
    for step in range(steps):
        for copy in fetches(arrays, buffer, sems, 0, step):
            copy.start()
    key_ref, value_ref, *doc_refs = [buffer.at[at] for at in range(len(arrays))]

    def group(step, carry):
        for copy in fetches(arrays, buffer, sems, 0, step):
            copy.wait()
        base = pl.multiple_of(step * TILE, TILE)
        for head in range(STEP):
            cols = pl.ds(pl.multiple_of((step * STEP + head) * HD, HD), HD)
            scores = scores_of(key_ref[:, cols], head_rows(doc_refs[:count], cols), low == 0)
            prob_grad = dot_nt(value_ref[:, cols], head_rows(doc_refs[count:], cols))
            top = jnp.max(scores, 0, keepdims=True)
            weights = jnp.exp(scores - top)
            total = jnp.sum(weights, 0, keepdims=True)
            mean = jnp.sum(weights * prob_grad, 0, keepdims=True) / total
            lse = top + jnp.log(total)
            for doc in range(count):
                cut = slice(doc * rows, (doc + 1) * rows)
                start = base + (low + doc) * steps * TILE
                out_ref[pl.ds(start + head, 1), :] = lse[:, cut]
                out_ref[pl.ds(start + STEP + head, 1), :] = mean[:, cut]
        return carry

    lax.fori_loop(0, steps, group, 0)
    if low:
        each = out_ref.shape[0] // GROUP
        out_ref[: before.shape[0], :] = before[...]
        for slot in range(2):
            value = offsets_ref[0, slot].astype(jnp.float32)
            at = each - TILE + slot * STEP
            out_ref[at : at + STEP, :] = jnp.full((STEP, rows), value, jnp.float32)
        for copy in range(1, GROUP):
            out_ref[copy * each : (copy + 1) * each, :] = out_ref[:each, :]


def merged(stat_ref, me, step, steps):
    stride = stat_ref.shape[0] // (3 * GROUP)
    sign = 1 - 2 * (me % 2)
    sign_real = sign.astype(jnp.float32)

    def tile(hops, row):
        place = me + GROUP + sign * hops
        return stat_ref[pl.ds(pl.multiple_of(place * stride + row, TILE), TILE), :]

    lse_rows, delta_rows = [], []
    for doc in DOCS:
        offsets = tile(doc, stride - TILE) * sign_real
        first, second = offsets[:STEP], offsets[STEP:]
        parts = []
        for hop in DOCS:
            name = -hop if (doc + hop) % 2 == 0 else hop
            stat = tile(doc + hop, (DOCS.index(name) * steps + step) * TILE)
            lse, mean = stat[:STEP], stat[STEP:]
            if hop:
                lse = jnp.where((first == hop) | (second == hop), lse, -FAR)
            parts.append((lse, mean))
        top = functools.reduce(jnp.maximum, [lse for lse, _ in parts])
        weights = [jnp.exp(lse - top) for lse, _ in parts]
        total = sum(weights)
        delta = sum(weight * mean for weight, (_, mean) in zip(weights, parts)) / total
        lse = top + jnp.log(total)
        if doc:
            lse = jnp.where((first == -doc) | (second == -doc), lse, FAR)
        lse_rows.append(lse)
        delta_rows.append(delta)
    return jnp.concatenate(lse_rows, 1), jnp.concatenate(delta_rows, 1)


def grads_kernel(first, replica_ref, *refs):
    count = len(DOCS)
    stat_refs, arrays = refs[:3], refs[3 : 5 + 2 * count]
    key_half, key_out, value_out = refs[-10:-7]
    stat_ref, buffer, key_buffer, value_buffer, stat_sem, sems, out_sem = refs[-7:]
    rows, features = arrays[0].shape
    half = key_half.shape[1]
    each = half // (STEP * HD)
    steps = features // (STEP * HD)
    size = stat_refs[0].shape[0]
    replica = replica_ref[0]

    above = 2 - 2 * (replica // GROUP % 2)
    stat_copies = [
        pltpu.make_async_copy(ref, stat_ref.at[pl.ds(pl.multiple_of(at * size, TILE), size), :], stat_sem)
        for at, ref in ((above, stat_refs[0]), (1, stat_refs[1]), (2 - above, stat_refs[2]))
    ]
    for copy in stat_copies:
        copy.start()
    for step in range(each):
        for copy in fetches(arrays, buffer, sems, first, step):
            copy.start()
    for copy in stat_copies:
        copy.wait()
    key_ref, value_ref, *doc_refs = [buffer.at[at] for at in range(len(arrays))]

    def group(step, carry):
        lse, delta = merged(stat_ref, replica % GROUP, first + step, steps)
        for copy in fetches(arrays, buffer, sems, first, step):
            copy.wait()
        for head in range(STEP):
            cols = pl.ds(pl.multiple_of((step * STEP + head) * HD, HD), HD)
            query_rows = head_rows(doc_refs[:count], cols)
            grad_rows = head_rows(doc_refs[count:], cols)
            scores = scores_of(key_ref[:, cols], query_rows, True)
            prob_grad = dot_nt(value_ref[:, cols], grad_rows)
            probs = jnp.exp(scores - lse[head : head + 1])
            score_grad = probs * (prob_grad - delta[head : head + 1]) * (HD ** (-0.5))
            key_total = dot_nn(score_grad.astype(jnp.bfloat16), query_rows)
            value_total = dot_nn(probs.astype(jnp.bfloat16), grad_rows)
            key_buffer[:, cols] = key_total.astype(jnp.bfloat16)
            value_buffer[:, cols] = value_total.astype(jnp.bfloat16)
        return carry

    lax.fori_loop(0, each, group, 0)
    cols = pl.ds(first * STEP * HD, half)
    out_copies = [
        pltpu.make_async_copy(key_buffer, key_half, out_sem.at[0]),
        pltpu.make_async_copy(key_buffer, key_out.at[:, cols], out_sem.at[1]),
        pltpu.make_async_copy(value_buffer, value_out.at[:, cols], out_sem.at[2]),
    ]
    for copy in out_copies:
        copy.start()
    for copy in out_copies:
        copy.wait()


def weight_kernel(low, mine_ref, inputs_ref, *refs):
    pieces, out_ref, grads_ref = refs[:4], refs[-2], refs[-1]
    wide = out_ref.shape[1]
    rows = pieces[0].shape[0]
    step = pl.program_id(0)
    here = pl.ds(pl.multiple_of(step * wide, HD), wide)
    whole = pl.ds(pl.multiple_of((low + step) * wide, HD), wide)
    for k, (ref, cols) in enumerate(zip(pieces, (whole, whole, here, here))):
        place = pl.multiple_of((mine_ref[0] ^ k) * rows, rows)
        grads_ref[pl.ds(place, rows), :] = ref[:, cols]
    out_ref[...] = dot_nn(inputs_ref[...], grads_ref[...]).astype(jnp.bfloat16)


def call_stats(low, high, partner_offsets, arrays, before):
    rows, features = arrays[0].shape
    heads = features // HD
    docs = len(DOCS)
    out_rows = high * heads // STEP * TILE if high < docs else GROUP * (docs * heads // STEP + 1) * TILE
    pairs = rows * rows * heads * (high - low)
    return pl.pallas_call(
        functools.partial(stats_kernel, low),
        in_specs=[pl.BlockSpec(memory_space=pltpu.SMEM)] + [ANY] * len(arrays) + [VMEM] * len(before),
        out_specs=VMEM,
        out_shape=jax.ShapeDtypeStruct((out_rows, rows), jnp.float32),
        scratch_shapes=[
            pltpu.VMEM((len(arrays), rows, features), jnp.bfloat16),
            pltpu.SemaphoreType.DMA((heads // STEP,)),
        ],
        compiler_params=PARAMS,
        cost_estimate=pl.CostEstimate(
            flops=4 * pairs * HD, bytes_accessed=2 * len(arrays) * rows * features, transcendentals=pairs
        ),
        name="stats",
    )(partner_offsets, *arrays, *before)


def call_grads(first, each, replica, stat_parts, arrays, held):
    rows, features = arrays[0].shape
    pairs = rows * rows * len(DOCS) * each * STEP
    half = (rows, each * STEP * HD)
    inputs = [replica, *stat_parts, *arrays]
    return pl.pallas_call(
        functools.partial(grads_kernel, first),
        in_specs=[pl.BlockSpec(memory_space=pltpu.SMEM)] + [ANY] * (len(inputs) - 1 + len(held)),
        out_specs=[ANY] * 3,
        out_shape=[
            jax.ShapeDtypeStruct(shape, jnp.bfloat16) for shape in (half, arrays[0].shape, arrays[0].shape)
        ],
        scratch_shapes=[
            pltpu.VMEM((3 * stat_parts[0].shape[0], rows), jnp.float32),
            pltpu.VMEM((len(arrays), *half), jnp.bfloat16),
            pltpu.VMEM(half, jnp.bfloat16),
            pltpu.VMEM(half, jnp.bfloat16),
            pltpu.SemaphoreType.DMA,
            pltpu.SemaphoreType.DMA((each,)),
            pltpu.SemaphoreType.DMA((3,)),
        ],
        input_output_aliases={len(inputs) + at: 1 + at for at in range(len(held))},
        compiler_params=PARAMS,
        cost_estimate=pl.CostEstimate(
            flops=8 * pairs * HD, bytes_accessed=2 * len(arrays) * half[0] * half[1], transcendentals=pairs
        ),
        name="grads",
    )(*inputs, *held)


def call_weight(half, mine, columns, pieces, held):
    features, part = pieces[0].shape[1], pieces[-1].shape[1]
    blocks = part // WIDE
    width, tokens = columns.shape
    return pl.pallas_call(
        functools.partial(weight_kernel, half * blocks),
        grid=(blocks,),
        in_specs=[pl.BlockSpec(memory_space=pltpu.SMEM)] + [VMEM] * (1 + len(pieces)) + [ANY] * len(held),
        out_specs=pl.BlockSpec((width, WIDE), lambda step: (0, step + half * blocks)),
        scratch_shapes=[pltpu.VMEM((tokens, WIDE), jnp.bfloat16)],
        out_shape=jax.ShapeDtypeStruct((width, features), jnp.bfloat16),
        input_output_aliases={2 + len(pieces): 0} if held else {},
        compiler_params=pltpu.CompilerParams(vmem_limit_bytes=24 << 20),
        cost_estimate=pl.CostEstimate(
            flops=2 * width * tokens * part, bytes_accessed=2 * part * (tokens + width), transcendentals=0
        ),
        name="weight",
    )(mine, *map(in_vmem, [columns, *pieces]), *held)


def local(layer_input, queries, key_vectors, value_vectors, output_grad, partner_offsets):
    rows, features = queries.shape
    steps = features // (HD * STEP)
    docs = len(DOCS)
    mine = lax.axis_index("fsdp").astype(jnp.int32).reshape(1)
    places = lax.axis_size("fsdp")

    others = [traded(array, "dp", 1, True) for array in (queries, output_grad)]
    firsts = [traded(array, "dp", 1, False) for array in (queries, output_grad)]
    near = list(zip(firsts, others))
    seconds = [traded(first, "dp", 1, True) for first in firsts]
    far = list(zip([traded(other, "dp", 1, False) for other in others], seconds))
    query_docs, grad_docs = (
        [array, *near[at], *far[at]] for at, array in enumerate((queries, output_grad))
    )

    own = [key_vectors, value_vectors]
    stats = call_stats(0, NEAR, partner_offsets, own + query_docs[:NEAR] + grad_docs[:NEAR], [])
    replica = lax.axis_index("dp").astype(jnp.int32).reshape(1)
    width = layer_input.shape[1] // places
    columns = layer_input.reshape(rows, places, width).transpose(1, 0, 2).reshape(places * rows, width)
    stats, replica, mine, columns = lax.optimization_barrier((stats, replica, mine, columns))
    stats = call_stats(NEAR, docs, partner_offsets, own + query_docs[NEAR:] + grad_docs[NEAR:], [stats])

    replicas = lax.axis_size("dp")
    groups = [list(range(low, low + GROUP)) for low in range(0, replicas, GROUP)]
    here = lax.all_to_all(stats, "dp", 0, 0, axis_index_groups=groups, tiled=True)
    stats, columns = lax.optimization_barrier((stats, columns))
    columns = lax.all_to_all(columns, "fsdp", 0, 0, tiled=True).T
    stat_parts = [traded(here, "dp", GROUP, False), here, traded(here, "dp", GROUP, True)]
    stat_parts[2], columns = lax.optimization_barrier((stat_parts[2], columns))

    each = steps // HALVES
    halves, held = [], []
    for half in range(HALVES):
        key_half, *held = call_grads(half * each, each, replica, stat_parts, own + query_docs + grad_docs, held)
        halves.append(key_half)
    key_grad, value_grad = held

    beside = swapped(key_grad, "fsdp", 1)
    held = []
    for half, key_half in enumerate(halves):
        across = swapped(key_half, "fsdp", 2)
        pieces = [key_grad, beside, across, swapped(across, "fsdp", 1)]
        held = [call_weight(half, mine, columns, pieces, held)]
    return held[0][None], value_grad


def solution(mesh):
    return jax.shard_map(
        local,
        mesh=mesh,
        in_specs=(
            P(("dp", "fsdp"), None),
            P(("dp", "fsdp"), None),
            P(("dp", "fsdp"), None),
            P(("dp", "fsdp"), None),
            P(("dp", "fsdp"), None),
            P("dp", None),
        ),
        out_specs=(P("dp", "fsdp", None), P(("dp", "fsdp"), None)),
        check_vma=False,
    )
```

```python
import functools

import jax
import jax.numpy as jnp
from jax import lax
from jax.experimental import pallas as pl
from jax.experimental.pallas import tpu as pltpu
from jax.sharding import PartitionSpec as P

HD = 128
DOCS = (0, 1, -1, 2, -2)
GROUP = 4
STEP = 4
TILE = 8
NEAR = 3
HALVES = 2
WIDE = 512
VMEM = pl.BlockSpec(memory_space=pltpu.VMEM)
ANY = pl.BlockSpec(memory_space=pl.ANY)
PARAMS = pltpu.CompilerParams(vmem_limit_bytes=24 << 20)
FAR = 1e30


def traded(value, axis, size, odd):
    count = lax.axis_size(axis)
    blocks = count // size
    pairs = []
    for source in range(count):
        block = source // size
        step = 1 if (block % 2 == 1) == odd else -1
        pairs.append((source, (block + step) % blocks * size + source % size))
    return lax.ppermute(value, axis, pairs)


def swapped(value, axis, mask):
    pairs = [(source, source ^ mask) for source in range(lax.axis_size(axis))]
    return lax.ppermute(value, axis, pairs)


def dot_nt(a, b):
    return lax.dot_general(a, b, (((1,), (1,)), ((), ())), preferred_element_type=jnp.float32)


def dot_nn(a, b):
    return lax.dot_general(a, b, (((1,), (0,)), ((), ())), preferred_element_type=jnp.float32)


def scores_of(keys, query_rows, own_first):
    scores = dot_nt(keys, query_rows) * (HD ** (-0.5))
    if not own_first:
        return scores
    rows = keys.shape[0]
    own = scores[:, :rows]
    key_at = lax.broadcasted_iota(jnp.int32, own.shape, 0)
    query_at = lax.broadcasted_iota(jnp.int32, own.shape, 1)
    own = jnp.where(key_at <= query_at, own, -FAR)
    return jnp.concatenate([own, scores[:, rows:]], 1)


def in_vmem(array):
    return pltpu.with_memory_space_constraint(array, pltpu.VMEM)


def head_rows(refs, cols):
    return jnp.concatenate([ref[:, cols] for ref in refs], 0)


def stats_kernel(low, offsets_ref, keys_ref, values_ref, *refs):
    count = (len(refs) - 1) // 2
    query_refs, grad_refs, out_ref = refs[:count], refs[count : 2 * count], refs[-1]
    rows, features = keys_ref.shape
    steps = features // (STEP * HD)

    def group(step, carry):
        base = pl.multiple_of(step * TILE, TILE)
        for head in range(STEP):
            cols = pl.ds(pl.multiple_of((step * STEP + head) * HD, HD), HD)
            scores = scores_of(keys_ref[:, cols], head_rows(query_refs, cols), low == 0)
            prob_grad = dot_nt(values_ref[:, cols], head_rows(grad_refs, cols))
            top = jnp.max(scores, 0, keepdims=True)
            weights = jnp.exp(scores - top)
            total = jnp.sum(weights, 0, keepdims=True)
            mean = jnp.sum(weights * prob_grad, 0, keepdims=True) / total
            lse = top + jnp.log(total)
            for doc in range(count):
                cut = slice(doc * rows, (doc + 1) * rows)
                start = base + (low + doc) * steps * TILE
                out_ref[pl.ds(start + head, 1), :] = lse[:, cut]
                out_ref[pl.ds(start + STEP + head, 1), :] = mean[:, cut]
        return carry

    lax.fori_loop(0, steps, group, 0)
    if low:
        before_ref = refs[2 * count]
        each = out_ref.shape[0] // GROUP
        out_ref[: before_ref.shape[0], :] = before_ref[...]
        for slot in range(2):
            value = offsets_ref[0, slot].astype(jnp.float32)
            at = each - TILE + slot * STEP
            out_ref[at : at + STEP, :] = jnp.full((STEP, rows), value, jnp.float32)
        for copy in range(1, GROUP):
            out_ref[copy * each : (copy + 1) * each, :] = out_ref[:each, :]


def merged(stat_ref, me, step, steps):
    stride = stat_ref.shape[0] // (3 * GROUP)
    sign = 1 - 2 * (me % 2)
    sign_real = sign.astype(jnp.float32)

    def tile(hops, row):
        place = me + GROUP + sign * hops
        return stat_ref[pl.ds(pl.multiple_of(place * stride + row, TILE), TILE), :]

    lse_rows, delta_rows = [], []
    for doc in DOCS:
        offsets = tile(doc, stride - TILE) * sign_real
        first, second = offsets[:STEP], offsets[STEP:]
        parts = []
        for hop in DOCS:
            name = -hop if (doc + hop) % 2 == 0 else hop
            stat = tile(doc + hop, (DOCS.index(name) * steps + step) * TILE)
            lse, mean = stat[:STEP], stat[STEP:]
            if hop:
                lse = jnp.where((first == hop) | (second == hop), lse, -FAR)
            parts.append((lse, mean))
        top = functools.reduce(jnp.maximum, [lse for lse, _ in parts])
        weights = [jnp.exp(lse - top) for lse, _ in parts]
        total = sum(weights)
        delta = sum(weight * mean for weight, (_, mean) in zip(weights, parts)) / total
        lse = top + jnp.log(total)
        if doc:
            lse = jnp.where((first == -doc) | (second == -doc), lse, FAR)
        lse_rows.append(lse)
        delta_rows.append(delta)
    return jnp.concatenate(lse_rows, 1), jnp.concatenate(delta_rows, 1)


def grads_kernel(first, replica_ref, *refs):
    count = len(DOCS)
    stat_refs, (keys_ref, values_ref), refs = refs[:3], refs[3:5], refs[5:]
    query_refs, grad_refs = refs[:count], refs[count : 2 * count]
    key_half, key_out, value_out, stat_ref, value_buffer, sems = refs[-6:]
    half = key_half.shape[1]
    each = half // (STEP * HD)
    steps = keys_ref.shape[1] // (STEP * HD)
    size = stat_refs[0].shape[0]
    replica = replica_ref[0]

    above = 2 - 2 * (replica // GROUP % 2)
    stat_copies = [
        pltpu.make_async_copy(ref, stat_ref.at[pl.ds(pl.multiple_of(place * size, TILE), size), :], sems.at[at])
        for at, (place, ref) in enumerate(zip((above, 1, 2 - above), stat_refs))
    ]
    for copy in stat_copies:
        copy.start()
    for copy in stat_copies:
        copy.wait()

    def group(at, carry):
        step = at + first
        lse, delta = merged(stat_ref, replica % GROUP, step, steps)
        for head in range(STEP):
            cols = pl.ds(pl.multiple_of((step * STEP + head) * HD, HD), HD)
            out_cols = pl.ds(pl.multiple_of((at * STEP + head) * HD, HD), HD)
            query_rows = head_rows(query_refs, cols)
            grad_rows = head_rows(grad_refs, cols)
            scores = scores_of(keys_ref[:, cols], query_rows, True)
            prob_grad = dot_nt(values_ref[:, cols], grad_rows)
            probs = jnp.exp(scores - lse[head : head + 1])
            score_grad = probs * (prob_grad - delta[head : head + 1]) * (HD ** (-0.5))
            key_total = dot_nn(score_grad.astype(jnp.bfloat16), query_rows)
            value_total = dot_nn(probs.astype(jnp.bfloat16), grad_rows)
            key_half[:, out_cols] = key_total.astype(jnp.bfloat16)
            value_buffer[:, out_cols] = value_total.astype(jnp.bfloat16)
        return carry

    lax.fori_loop(0, each, group, 0)
    cols = pl.ds(first * STEP * HD, half)
    out_copies = [
        pltpu.make_async_copy(key_half, key_out.at[:, cols], sems.at[3]),
        pltpu.make_async_copy(value_buffer, value_out.at[:, cols], sems.at[4]),
    ]
    for copy in out_copies:
        copy.start()
    for copy in out_copies:
        copy.wait()


def spread_kernel(input_ref, out_ref, sems):
    rows, features = input_ref.shape
    width = out_ref.shape[1]
    copies = [
        pltpu.make_async_copy(
            input_ref.at[:, pl.ds(place * width, width)], out_ref.at[pl.ds(place * rows, rows), :], sems.at[place]
        )
        for place in range(features // width)
    ]
    for copy in copies:
        copy.start()
    for copy in copies:
        copy.wait()


def weight_kernel(low, mine_ref, inputs_ref, *refs):
    pieces, out_ref, turned_ref, grads_ref = refs[:4], *refs[-3:]
    wide = out_ref.shape[1]
    rows = pieces[0].shape[0]
    step = pl.program_id(0)

    @pl.when(step == 0)
    def _():
        turned_ref[...] = inputs_ref[...].T

    here = pl.ds(pl.multiple_of(step * wide, HD), wide)
    whole = pl.ds(pl.multiple_of((low + step) * wide, HD), wide)
    for k, (ref, cols) in enumerate(zip(pieces, (here, whole, here, here))):
        place = pl.multiple_of((mine_ref[0] ^ k) * rows, rows)
        grads_ref[pl.ds(place, rows), :] = ref[:, cols]
    out_ref[...] = dot_nn(turned_ref[...], grads_ref[...]).astype(jnp.bfloat16)


def call_stats(low, high, partner_offsets, arrays, before):
    rows, features = arrays[0].shape
    heads = features // HD
    docs = len(DOCS)
    out_rows = high * heads // STEP * TILE if high < docs else GROUP * (docs * heads // STEP + 1) * TILE
    pairs = rows * rows * heads * (high - low)
    return pl.pallas_call(
        functools.partial(stats_kernel, low),
        in_specs=[pl.BlockSpec(memory_space=pltpu.SMEM)] + [VMEM] * (len(arrays) + len(before)),
        out_specs=VMEM,
        out_shape=pltpu.VMEM((out_rows, rows), jnp.float32),
        compiler_params=PARAMS,
        cost_estimate=pl.CostEstimate(
            flops=4 * pairs * HD, bytes_accessed=2 * len(arrays) * rows * features, transcendentals=pairs
        ),
        name="stats",
    )(partner_offsets, *map(in_vmem, arrays), *map(in_vmem, before))


def call_grads(first, each, replica, stat_parts, arrays, held):
    rows, features = arrays[0].shape
    pairs = rows * rows * len(DOCS) * each * STEP
    half = (rows, each * STEP * HD)
    whole = jax.ShapeDtypeStruct((rows, features), jnp.bfloat16)
    count = 1 + len(stat_parts) + len(arrays)
    return pl.pallas_call(
        functools.partial(grads_kernel, first),
        in_specs=[pl.BlockSpec(memory_space=pltpu.SMEM)]
        + [ANY] * len(stat_parts)
        + [VMEM] * len(arrays)
        + [ANY] * len(held),
        out_specs=[VMEM, ANY, ANY],
        out_shape=[pltpu.VMEM(half, jnp.bfloat16), whole, whole],
        scratch_shapes=[
            pltpu.VMEM((3 * stat_parts[0].shape[0], rows), jnp.float32),
            pltpu.VMEM(half, jnp.bfloat16),
            pltpu.SemaphoreType.DMA((5,)),
        ],
        input_output_aliases={count + at: 1 + at for at in range(len(held))},
        compiler_params=PARAMS,
        cost_estimate=pl.CostEstimate(
            flops=8 * pairs * HD, bytes_accessed=2 * len(arrays) * half[0] * half[1], transcendentals=pairs
        ),
        name="grads",
    )(replica, *stat_parts, *map(in_vmem, arrays), *held)


def call_spread(layer_input, places):
    rows, features = layer_input.shape
    return pl.pallas_call(
        spread_kernel,
        in_specs=[ANY],
        out_specs=ANY,
        out_shape=jax.ShapeDtypeStruct((places * rows, features // places), jnp.bfloat16),
        scratch_shapes=[pltpu.SemaphoreType.DMA((places,))],
        compiler_params=PARAMS,
        cost_estimate=pl.CostEstimate(flops=0, bytes_accessed=4 * rows * features, transcendentals=0),
        name="spread",
    )(layer_input)


def call_weight(half, mine, columns, pieces, held):
    features, part = pieces[1].shape[1], pieces[0].shape[1]
    blocks = part // WIDE
    tokens, width = columns.shape
    return pl.pallas_call(
        functools.partial(weight_kernel, half * blocks),
        grid=(blocks,),
        in_specs=[pl.BlockSpec(memory_space=pltpu.SMEM)] + [VMEM] * (1 + len(pieces)) + [ANY] * len(held),
        out_specs=pl.BlockSpec((width, WIDE), lambda step: (0, step + half * blocks)),
        out_shape=jax.ShapeDtypeStruct((width, features), jnp.bfloat16),
        scratch_shapes=[pltpu.VMEM((width, tokens), jnp.bfloat16), pltpu.VMEM((tokens, WIDE), jnp.bfloat16)],
        input_output_aliases={2 + len(pieces): 0} if held else {},
        compiler_params=PARAMS,
        cost_estimate=pl.CostEstimate(
            flops=2 * width * tokens * part, bytes_accessed=2 * part * (tokens + width), transcendentals=0
        ),
        name="weight",
    )(mine, *map(in_vmem, [columns, *pieces]), *held)


def local(layer_input, queries, key_vectors, value_vectors, output_grad, partner_offsets):
    rows, features = queries.shape
    steps = features // (HD * STEP)
    docs = len(DOCS)
    places = lax.axis_size("fsdp")
    mine = lax.axis_index("fsdp").astype(jnp.int32).reshape(1)
    replica = lax.axis_index("dp").astype(jnp.int32).reshape(1)
    queries, mine, replica = lax.optimization_barrier((queries, mine, replica))

    others = [traded(array, "dp", 1, True) for array in (queries, output_grad)]
    firsts = [traded(array, "dp", 1, False) for array in (queries, output_grad)]
    near = list(zip(firsts, others))
    seconds = [traded(first, "dp", 1, True) for first in firsts]
    far = list(zip([traded(other, "dp", 1, False) for other in others], seconds))
    query_docs, grad_docs = (
        [array, *near[at], *far[at]] for at, array in enumerate((queries, output_grad))
    )

    own = [key_vectors, value_vectors]
    stats = call_stats(0, NEAR, partner_offsets, own + query_docs[:NEAR] + grad_docs[:NEAR], [])
    columns = call_spread(layer_input, places)
    stats, columns = lax.optimization_barrier((stats, columns))
    columns = lax.all_to_all(columns, "fsdp", 0, 0, tiled=True)
    stats = call_stats(NEAR, docs, partner_offsets, own + query_docs[NEAR:] + grad_docs[NEAR:], [stats])

    replicas = lax.axis_size("dp")
    groups = [list(range(low, low + GROUP)) for low in range(0, replicas, GROUP)]
    here = lax.all_to_all(stats, "dp", 0, 0, axis_index_groups=groups, tiled=True)
    after_even = traded(here, "dp", GROUP, False)
    here, columns = lax.optimization_barrier((here, columns))
    stat_parts = [after_even, here, traded(here, "dp", GROUP, True)]

    each = steps // HALVES
    halves, held = [], []
    for half in range(HALVES):
        key_half, *held = call_grads(half * each, each, replica, stat_parts, own + query_docs + grad_docs, held)
        halves.append(key_half)
    key_grad, value_grad = held

    beside = swapped(key_grad, "fsdp", 1)
    held = []
    for half, key_half in enumerate(halves):
        across = swapped(key_half, "fsdp", 2)
        pieces = [key_half, beside, across, swapped(across, "fsdp", 1)]
        held = [call_weight(half, mine, columns, pieces, held)]
    return held[0][None], value_grad


def solution(mesh):
    return jax.shard_map(
        local,
        mesh=mesh,
        in_specs=(
            P(("dp", "fsdp"), None),
            P(("dp", "fsdp"), None),
            P(("dp", "fsdp"), None),
            P(("dp", "fsdp"), None),
            P(("dp", "fsdp"), None),
            P("dp", None),
        ),
        out_specs=(P("dp", "fsdp", None), P(("dp", "fsdp"), None)),
        check_vma=False,
    )
```

```python
import functools

import jax
import jax.numpy as jnp
from jax import lax
from jax.experimental import pallas as pl
from jax.experimental.pallas import tpu as pltpu
from jax.sharding import PartitionSpec as P

HD = 128
DOCS = (0, 1, -1, 2, -2)
GROUP = 4
STEP = 4
TILE = 8
NEAR = 3
HALVES = 2
WIDE = 512
VMEM = pl.BlockSpec(memory_space=pltpu.VMEM)
ANY = pl.BlockSpec(memory_space=pl.ANY)
PARAMS = pltpu.CompilerParams(vmem_limit_bytes=24 << 20)
FAR = 1e30


def traded(value, axis, size, odd):
    count = lax.axis_size(axis)
    blocks = count // size
    pairs = []
    for source in range(count):
        block = source // size
        step = 1 if (block % 2 == 1) == odd else -1
        pairs.append((source, (block + step) % blocks * size + source % size))
    return lax.ppermute(value, axis, pairs)


def swapped(value, axis, mask):
    pairs = [(source, source ^ mask) for source in range(lax.axis_size(axis))]
    return lax.ppermute(value, axis, pairs)


def dot_nt(a, b):
    return lax.dot_general(a, b, (((1,), (1,)), ((), ())), preferred_element_type=jnp.float32)


def dot_nn(a, b):
    return lax.dot_general(a, b, (((1,), (0,)), ((), ())), preferred_element_type=jnp.float32)


def scores_of(keys, query_rows, own_first):
    scores = dot_nt(keys, query_rows) * (HD ** (-0.5))
    if not own_first:
        return scores
    rows = keys.shape[0]
    own = scores[:, :rows]
    key_at = lax.broadcasted_iota(jnp.int32, own.shape, 0)
    query_at = lax.broadcasted_iota(jnp.int32, own.shape, 1)
    own = jnp.where(key_at <= query_at, own, -FAR)
    return jnp.concatenate([own, scores[:, rows:]], 1)


def in_vmem(array):
    return pltpu.with_memory_space_constraint(array, pltpu.VMEM)


def head_rows(refs, cols):
    return jnp.concatenate([ref[:, cols] for ref in refs], 0)


def stats_kernel(low, offsets_ref, keys_ref, values_ref, *refs):
    count = (len(refs) - 1) // 2
    query_refs, grad_refs, out_ref = refs[:count], refs[count : 2 * count], refs[-1]
    rows, features = keys_ref.shape
    steps = features // (STEP * HD)

    def group(step, carry):
        base = pl.multiple_of(step * TILE, TILE)
        for head in range(STEP):
            cols = pl.ds(pl.multiple_of((step * STEP + head) * HD, HD), HD)
            scores = scores_of(keys_ref[:, cols], head_rows(query_refs, cols), low == 0)
            prob_grad = dot_nt(values_ref[:, cols], head_rows(grad_refs, cols))
            top = jnp.max(scores, 0, keepdims=True)
            weights = jnp.exp(scores - top)
            total = jnp.sum(weights, 0, keepdims=True)
            mean = jnp.sum(weights * prob_grad, 0, keepdims=True) / total
            lse = top + jnp.log(total)
            for doc in range(count):
                cut = slice(doc * rows, (doc + 1) * rows)
                start = base + (low + doc) * steps * TILE
                out_ref[pl.ds(start + head, 1), :] = lse[:, cut]
                out_ref[pl.ds(start + STEP + head, 1), :] = mean[:, cut]
        return carry

    lax.fori_loop(0, steps, group, 0)
    if low:
        before_ref = refs[2 * count]
        each = out_ref.shape[0] // GROUP
        out_ref[: before_ref.shape[0], :] = before_ref[...]
        for slot in range(2):
            value = offsets_ref[0, slot].astype(jnp.float32)
            at = each - TILE + slot * STEP
            out_ref[at : at + STEP, :] = jnp.full((STEP, rows), value, jnp.float32)
        for copy in range(1, GROUP):
            out_ref[copy * each : (copy + 1) * each, :] = out_ref[:each, :]


def merged(stat_ref, me, step, steps):
    stride = stat_ref.shape[0] // (3 * GROUP)
    sign = 1 - 2 * (me % 2)
    sign_real = sign.astype(jnp.float32)

    def tile(hops, row):
        place = me + GROUP + sign * hops
        return stat_ref[pl.ds(pl.multiple_of(place * stride + row, TILE), TILE), :]

    lse_rows, delta_rows = [], []
    for doc in DOCS:
        offsets = tile(doc, stride - TILE) * sign_real
        first, second = offsets[:STEP], offsets[STEP:]
        parts = []
        for hop in DOCS:
            name = -hop if (doc + hop) % 2 == 0 else hop
            stat = tile(doc + hop, (DOCS.index(name) * steps + step) * TILE)
            lse, mean = stat[:STEP], stat[STEP:]
            if hop:
                lse = jnp.where((first == hop) | (second == hop), lse, -FAR)
            parts.append((lse, mean))
        top = functools.reduce(jnp.maximum, [lse for lse, _ in parts])
        weights = [jnp.exp(lse - top) for lse, _ in parts]
        total = sum(weights)
        delta = sum(weight * mean for weight, (_, mean) in zip(weights, parts)) / total
        lse = top + jnp.log(total)
        if doc:
            lse = jnp.where((first == -doc) | (second == -doc), lse, FAR)
        lse_rows.append(lse)
        delta_rows.append(delta)
    return jnp.concatenate(lse_rows, 1), jnp.concatenate(delta_rows, 1)


def grads_kernel(first, replica_ref, *refs):
    count = len(DOCS)
    stat_refs, (keys_ref, values_ref), refs = refs[:3], refs[3:5], refs[5:]
    query_refs, grad_refs = refs[:count], refs[count : 2 * count]
    key_half, key_out, value_out, stat_ref, value_buffer, sems = refs[-6:]
    half = key_half.shape[1]
    each = half // (STEP * HD)
    steps = keys_ref.shape[1] // (STEP * HD)
    size = stat_refs[0].shape[0]
    replica = replica_ref[0]

    above = 2 - 2 * (replica // GROUP % 2)
    for place, ref in zip((2 - above, 1, above), stat_refs):
        stat_ref[pl.ds(pl.multiple_of(place * size, TILE), size), :] = ref[...]

    def writes(at):
        cols = pl.ds(pl.multiple_of((at + first) * STEP * HD, HD), STEP * HD)
        part = pl.ds(pl.multiple_of(at * STEP * HD, HD), STEP * HD)
        return [
            pltpu.make_async_copy(source.at[:, part], target.at[:, cols], sems.at[kind, at])
            for kind, (source, target) in enumerate(((key_half, key_out), (value_buffer, value_out)))
        ]

    def group(at, carry):
        step = at + first
        lse, delta = merged(stat_ref, replica % GROUP, step, steps)
        for head in range(STEP):
            cols = pl.ds(pl.multiple_of((step * STEP + head) * HD, HD), HD)
            out_cols = pl.ds(pl.multiple_of((at * STEP + head) * HD, HD), HD)
            query_rows = head_rows(query_refs, cols)
            grad_rows = head_rows(grad_refs, cols)
            scores = scores_of(keys_ref[:, cols], query_rows, True)
            prob_grad = dot_nt(values_ref[:, cols], grad_rows)
            probs = jnp.exp(scores - lse[head : head + 1])
            score_grad = probs * (prob_grad - delta[head : head + 1]) * (HD ** (-0.5))
            key_total = dot_nn(score_grad.astype(jnp.bfloat16), query_rows)
            value_total = dot_nn(probs.astype(jnp.bfloat16), grad_rows)
            key_half[:, out_cols] = key_total.astype(jnp.bfloat16)
            value_buffer[:, out_cols] = value_total.astype(jnp.bfloat16)
        for copy in writes(at):
            copy.start()
        return carry

    lax.fori_loop(0, each, group, 0)
    for at in range(each):
        for copy in writes(at):
            copy.wait()


def spread_kernel(input_ref, out_ref, sems):
    rows, features = input_ref.shape
    width = out_ref.shape[1]
    copies = [
        pltpu.make_async_copy(
            input_ref.at[:, pl.ds(place * width, width)], out_ref.at[pl.ds(place * rows, rows), :], sems.at[place]
        )
        for place in range(features // width)
    ]
    for copy in copies:
        copy.start()
    for copy in copies:
        copy.wait()


def weight_kernel(low, mine_ref, inputs_ref, *refs):
    pieces, out_ref, turned_ref, grads_ref = refs[:4], *refs[-3:]
    wide = out_ref.shape[1]
    rows = pieces[0].shape[0]
    step = pl.program_id(0)

    @pl.when(step == 0)
    def _():
        turned_ref[...] = inputs_ref[...].T

    here = pl.ds(pl.multiple_of(step * wide, HD), wide)
    whole = pl.ds(pl.multiple_of((low + step) * wide, HD), wide)
    for k, (ref, cols) in enumerate(zip(pieces, (here, whole, here, here))):
        place = pl.multiple_of((mine_ref[0] ^ k) * rows, rows)
        grads_ref[pl.ds(place, rows), :] = ref[:, cols]
    out_ref[...] = dot_nn(turned_ref[...], grads_ref[...]).astype(jnp.bfloat16)


def call_stats(low, high, partner_offsets, arrays, before):
    rows, features = arrays[0].shape
    heads = features // HD
    docs = len(DOCS)
    out_rows = high * heads // STEP * TILE if high < docs else GROUP * (docs * heads // STEP + 1) * TILE
    pairs = rows * rows * heads * (high - low)
    return pl.pallas_call(
        functools.partial(stats_kernel, low),
        in_specs=[pl.BlockSpec(memory_space=pltpu.SMEM)] + [VMEM] * (len(arrays) + len(before)),
        out_specs=VMEM,
        out_shape=pltpu.VMEM((out_rows, rows), jnp.float32),
        compiler_params=PARAMS,
        cost_estimate=pl.CostEstimate(
            flops=4 * pairs * HD, bytes_accessed=2 * len(arrays) * rows * features, transcendentals=pairs
        ),
        name="stats",
    )(partner_offsets, *map(in_vmem, arrays), *map(in_vmem, before))


def call_grads(first, each, replica, stat_parts, arrays, held):
    rows, features = arrays[0].shape
    pairs = rows * rows * len(DOCS) * each * STEP
    half = (rows, each * STEP * HD)
    whole = jax.ShapeDtypeStruct((rows, features), jnp.bfloat16)
    count = 1 + len(stat_parts) + len(arrays)
    return pl.pallas_call(
        functools.partial(grads_kernel, first),
        in_specs=[pl.BlockSpec(memory_space=pltpu.SMEM)]
        + [VMEM] * (len(stat_parts) + len(arrays))
        + [ANY] * len(held),
        out_specs=[VMEM, ANY, ANY],
        out_shape=[pltpu.VMEM(half, jnp.bfloat16), whole, whole],
        scratch_shapes=[
            pltpu.VMEM((3 * stat_parts[0].shape[0], rows), jnp.float32),
            pltpu.VMEM(half, jnp.bfloat16),
            pltpu.SemaphoreType.DMA((2, each)),
        ],
        input_output_aliases={count + at: 1 + at for at in range(len(held))},
        compiler_params=PARAMS,
        cost_estimate=pl.CostEstimate(
            flops=8 * pairs * HD, bytes_accessed=2 * len(arrays) * half[0] * half[1], transcendentals=pairs
        ),
        name="grads",
    )(replica, *map(in_vmem, [*stat_parts, *arrays]), *held)


def call_spread(layer_input, places):
    rows, features = layer_input.shape
    return pl.pallas_call(
        spread_kernel,
        in_specs=[ANY],
        out_specs=ANY,
        out_shape=jax.ShapeDtypeStruct((places * rows, features // places), jnp.bfloat16),
        scratch_shapes=[pltpu.SemaphoreType.DMA((places,))],
        compiler_params=PARAMS,
        cost_estimate=pl.CostEstimate(flops=0, bytes_accessed=4 * rows * features, transcendentals=0),
        name="spread",
    )(layer_input)


def call_weight(half, mine, columns, pieces, held):
    features, part = pieces[1].shape[1], pieces[0].shape[1]
    blocks = part // WIDE
    tokens, width = columns.shape
    return pl.pallas_call(
        functools.partial(weight_kernel, half * blocks),
        grid=(blocks,),
        in_specs=[pl.BlockSpec(memory_space=pltpu.SMEM)] + [VMEM] * (1 + len(pieces)) + [ANY] * len(held),
        out_specs=pl.BlockSpec((width, WIDE), lambda step: (0, step + half * blocks)),
        out_shape=jax.ShapeDtypeStruct((width, features), jnp.bfloat16),
        scratch_shapes=[pltpu.VMEM((width, tokens), jnp.bfloat16), pltpu.VMEM((tokens, WIDE), jnp.bfloat16)],
        input_output_aliases={2 + len(pieces): 0} if held else {},
        compiler_params=PARAMS,
        cost_estimate=pl.CostEstimate(
            flops=2 * width * tokens * part, bytes_accessed=2 * part * (tokens + width), transcendentals=0
        ),
        name="weight",
    )(mine, *map(in_vmem, [columns, *pieces]), *held)


def local(layer_input, queries, key_vectors, value_vectors, output_grad, partner_offsets):
    rows, features = queries.shape
    steps = features // (HD * STEP)
    docs = len(DOCS)
    places = lax.axis_size("fsdp")
    mine = lax.axis_index("fsdp").astype(jnp.int32).reshape(1)
    replica = lax.axis_index("dp").astype(jnp.int32).reshape(1)
    queries, mine, replica = lax.optimization_barrier((queries, mine, replica))

    others = [traded(array, "dp", 1, True) for array in (queries, output_grad)]
    firsts = [traded(array, "dp", 1, False) for array in (queries, output_grad)]
    near = list(zip(firsts, others))
    seconds = [traded(first, "dp", 1, True) for first in firsts]
    far = list(zip([traded(other, "dp", 1, False) for other in others], seconds))
    query_docs, grad_docs = (
        [array, *near[at], *far[at]] for at, array in enumerate((queries, output_grad))
    )

    own = [key_vectors, value_vectors]
    stats = call_stats(0, NEAR, partner_offsets, own + query_docs[:NEAR] + grad_docs[:NEAR], [])
    columns = call_spread(layer_input, places)
    stats, columns = lax.optimization_barrier((stats, columns))
    columns = lax.all_to_all(columns, "fsdp", 0, 0, tiled=True)
    stats = call_stats(NEAR, docs, partner_offsets, own + query_docs[NEAR:] + grad_docs[NEAR:], [stats])

    replicas = lax.axis_size("dp")
    groups = [list(range(low, low + GROUP)) for low in range(0, replicas, GROUP)]
    here = lax.all_to_all(stats, "dp", 0, 0, axis_index_groups=groups, tiled=True)
    after_odd = traded(here, "dp", GROUP, True)
    here, columns = lax.optimization_barrier((here, columns))
    stat_parts = [after_odd, here, traded(here, "dp", GROUP, False)]

    each = steps // HALVES
    halves, held = [], []
    for half in range(HALVES):
        key_half, *held = call_grads(half * each, each, replica, stat_parts, own + query_docs + grad_docs, held)
        halves.append(key_half)
    key_grad, value_grad = held

    beside = swapped(key_grad, "fsdp", 1)
    held = []
    for half, key_half in enumerate(halves):
        across = swapped(key_half, "fsdp", 2)
        pieces = [key_half, beside, across, swapped(across, "fsdp", 1)]
        held = [call_weight(half, mine, columns, pieces, held)]
    return held[0][None], value_grad


def solution(mesh):
    return jax.shard_map(
        local,
        mesh=mesh,
        in_specs=(
            P(("dp", "fsdp"), None),
            P(("dp", "fsdp"), None),
            P(("dp", "fsdp"), None),
            P(("dp", "fsdp"), None),
            P(("dp", "fsdp"), None),
            P("dp", None),
        ),
        out_specs=(P("dp", "fsdp", None), P(("dp", "fsdp"), None)),
        check_vma=False,
    )
```

```python
import functools

import jax
import jax.numpy as jnp
from jax import lax
from jax.experimental import pallas as pl
from jax.experimental.pallas import tpu as pltpu
from jax.sharding import PartitionSpec as P

HD = 128
DOCS = (0, 1, -1, 2, -2)
GROUP = 4
STEP = 4
TILE = 8
NEAR = 3
HALVES = 2
WIDE = 512
VMEM = pl.BlockSpec(memory_space=pltpu.VMEM)
ANY = pl.BlockSpec(memory_space=pl.ANY)
PARAMS = pltpu.CompilerParams(vmem_limit_bytes=24 << 20)
FAR = 1e30


def traded(value, axis, size, odd):
    count = lax.axis_size(axis)
    blocks = count // size
    pairs = []
    for source in range(count):
        block = source // size
        step = 1 if (block % 2 == 1) == odd else -1
        pairs.append((source, (block + step) % blocks * size + source % size))
    return lax.ppermute(value, axis, pairs)


def swapped(value, axis, mask):
    pairs = [(source, source ^ mask) for source in range(lax.axis_size(axis))]
    return lax.ppermute(value, axis, pairs)


def dot_nt(a, b):
    return lax.dot_general(a, b, (((1,), (1,)), ((), ())), preferred_element_type=jnp.float32)


def dot_nn(a, b):
    return lax.dot_general(a, b, (((1,), (0,)), ((), ())), preferred_element_type=jnp.float32)


def scores_of(keys, query_rows, own_first):
    scores = dot_nt(keys, query_rows) * (HD ** (-0.5))
    if not own_first:
        return scores
    rows = keys.shape[0]
    own = scores[:, :rows]
    key_at = lax.broadcasted_iota(jnp.int32, own.shape, 0)
    query_at = lax.broadcasted_iota(jnp.int32, own.shape, 1)
    own = jnp.where(key_at <= query_at, own, -FAR)
    return jnp.concatenate([own, scores[:, rows:]], 1)


def in_vmem(array):
    return pltpu.with_memory_space_constraint(array, pltpu.VMEM)


def head_rows(refs, cols):
    return jnp.concatenate([ref[:, cols] for ref in refs], 0)


def stats_kernel(low, offsets_ref, keys_ref, values_ref, *refs):
    count = (len(refs) - 1) // 2
    query_refs, grad_refs, out_ref = refs[:count], refs[count : 2 * count], refs[-1]
    rows, features = keys_ref.shape
    steps = features // (STEP * HD)

    def group(step, carry):
        base = pl.multiple_of(step * TILE, TILE)
        for head in range(STEP):
            cols = pl.ds(pl.multiple_of((step * STEP + head) * HD, HD), HD)
            scores = scores_of(keys_ref[:, cols], head_rows(query_refs, cols), low == 0)
            prob_grad = dot_nt(values_ref[:, cols], head_rows(grad_refs, cols))
            top = jnp.max(scores, 0, keepdims=True)
            weights = jnp.exp(scores - top)
            total = jnp.sum(weights, 0, keepdims=True)
            mean = jnp.sum(weights * prob_grad, 0, keepdims=True) / total
            lse = top + jnp.log(total)
            for doc in range(count):
                cut = slice(doc * rows, (doc + 1) * rows)
                start = base + (low + doc) * steps * TILE
                out_ref[pl.ds(start + head, 1), :] = lse[:, cut]
                out_ref[pl.ds(start + STEP + head, 1), :] = mean[:, cut]
        return carry

    lax.fori_loop(0, steps, group, 0)
    if low:
        before_ref = refs[2 * count]
        each = out_ref.shape[0] // GROUP
        out_ref[: before_ref.shape[0], :] = before_ref[...]
        for slot in range(2):
            value = offsets_ref[0, slot].astype(jnp.float32)
            at = each - TILE + slot * STEP
            out_ref[at : at + STEP, :] = jnp.full((STEP, rows), value, jnp.float32)
        for copy in range(1, GROUP):
            out_ref[copy * each : (copy + 1) * each, :] = out_ref[:each, :]


def merged(stat_ref, me, step, steps):
    stride = stat_ref.shape[0] // (3 * GROUP)
    sign = 1 - 2 * (me % 2)
    sign_real = sign.astype(jnp.float32)

    def tile(hops, row):
        place = me + GROUP + sign * hops
        return stat_ref[pl.ds(pl.multiple_of(place * stride + row, TILE), TILE), :]

    lse_rows, delta_rows = [], []
    for doc in DOCS:
        offsets = tile(doc, stride - TILE) * sign_real
        first, second = offsets[:STEP], offsets[STEP:]
        parts = []
        for hop in DOCS:
            name = -hop if (doc + hop) % 2 == 0 else hop
            stat = tile(doc + hop, (DOCS.index(name) * steps + step) * TILE)
            lse, mean = stat[:STEP], stat[STEP:]
            if hop:
                lse = jnp.where((first == hop) | (second == hop), lse, -FAR)
            parts.append((lse, mean))
        top = functools.reduce(jnp.maximum, [lse for lse, _ in parts])
        weights = [jnp.exp(lse - top) for lse, _ in parts]
        total = sum(weights)
        delta = sum(weight * mean for weight, (_, mean) in zip(weights, parts)) / total
        lse = top + jnp.log(total)
        if doc:
            lse = jnp.where((first == -doc) | (second == -doc), lse, FAR)
        lse_rows.append(lse)
        delta_rows.append(delta)
    return jnp.concatenate(lse_rows, 1), jnp.concatenate(delta_rows, 1)


def grads_kernel(first, replica_ref, *refs):
    count = len(DOCS)
    stat_refs, (keys_ref, values_ref), refs = refs[:3], refs[3:5], refs[5:]
    query_refs, grad_refs = refs[:count], refs[count : 2 * count]
    key_half, value_out, stat_ref = refs[-3:]
    skip = value_out.shape[1] - key_half.shape[1]
    if skip:
        value_out[:, :skip] = refs[-4][...]
    half = key_half.shape[1]
    each = half // (STEP * HD)
    steps = keys_ref.shape[1] // (STEP * HD)
    size = stat_refs[0].shape[0]
    replica = replica_ref[0]

    above = 2 - 2 * (replica // GROUP % 2)
    for place, ref in zip((2 - above, 1, above), stat_refs):
        stat_ref[pl.ds(pl.multiple_of(place * size, TILE), size), :] = ref[...]

    def group(at, carry):
        step = at + first
        lse, delta = merged(stat_ref, replica % GROUP, step, steps)
        for head in range(STEP):
            cols = pl.ds(pl.multiple_of((step * STEP + head) * HD, HD), HD)
            out_cols = pl.ds(pl.multiple_of((at * STEP + head) * HD, HD), HD)
            query_rows = head_rows(query_refs, cols)
            grad_rows = head_rows(grad_refs, cols)
            scores = scores_of(keys_ref[:, cols], query_rows, True)
            prob_grad = dot_nt(values_ref[:, cols], grad_rows)
            probs = jnp.exp(scores - lse[head : head + 1])
            score_grad = probs * (prob_grad - delta[head : head + 1]) * (HD ** (-0.5))
            key_total = dot_nn(score_grad.astype(jnp.bfloat16), query_rows)
            value_total = dot_nn(probs.astype(jnp.bfloat16), grad_rows)
            key_half[:, out_cols] = key_total.astype(jnp.bfloat16)
            value_cols = pl.ds(pl.multiple_of(skip + (at * STEP + head) * HD, HD), HD)
            value_out[:, value_cols] = value_total.astype(jnp.bfloat16)
        return carry

    lax.fori_loop(0, each, group, 0)


def spread_kernel(input_ref, out_ref, sems):
    rows, features = input_ref.shape
    width = out_ref.shape[1]
    copies = [
        pltpu.make_async_copy(
            input_ref.at[:, pl.ds(place * width, width)], out_ref.at[pl.ds(place * rows, rows), :], sems.at[place]
        )
        for place in range(features // width)
    ]
    for copy in copies:
        copy.start()
    for copy in copies:
        copy.wait()


def weight_kernel(saves, mine_ref, inputs_ref, *refs):
    pieces, (turned_ref, grads_ref, sem) = refs[:4], refs[-3:]
    out_ref = refs[-5] if saves else refs[-4]
    wide = out_ref.shape[1]
    rows = pieces[0].shape[0]
    step = pl.program_id(0)
    copy = pltpu.make_async_copy(refs[4], refs[-4], sem) if saves else None

    @pl.when(step == 0)
    def _():
        if saves:
            copy.start()
        turned_ref[...] = inputs_ref[...].T

    cols = pl.ds(pl.multiple_of(step * wide, HD), wide)
    for k, ref in enumerate(pieces):
        place = pl.multiple_of((mine_ref[0] ^ k) * rows, rows)
        grads_ref[pl.ds(place, rows), :] = ref[:, cols]
    out_ref[...] = dot_nn(turned_ref[...], grads_ref[...]).astype(jnp.bfloat16)

    if saves:

        @pl.when(step == pl.num_programs(0) - 1)
        def _():
            copy.wait()


def call_stats(low, high, partner_offsets, arrays, before):
    rows, features = arrays[0].shape
    heads = features // HD
    docs = len(DOCS)
    out_rows = high * heads // STEP * TILE if high < docs else GROUP * (docs * heads // STEP + 1) * TILE
    pairs = rows * rows * heads * (high - low)
    return pl.pallas_call(
        functools.partial(stats_kernel, low),
        in_specs=[pl.BlockSpec(memory_space=pltpu.SMEM)] + [VMEM] * (len(arrays) + len(before)),
        out_specs=VMEM,
        out_shape=pltpu.VMEM((out_rows, rows), jnp.float32),
        compiler_params=PARAMS,
        cost_estimate=pl.CostEstimate(
            flops=4 * pairs * HD, bytes_accessed=2 * len(arrays) * rows * features, transcendentals=pairs
        ),
        name="stats",
    )(partner_offsets, *map(in_vmem, arrays), *map(in_vmem, before))


def call_grads(first, each, replica, stat_parts, arrays, before):
    rows, features = arrays[0].shape
    pairs = rows * rows * len(DOCS) * each * STEP
    half = (rows, each * STEP * HD)
    whole = (rows, (len(before) + 1) * half[1])
    inputs = [*stat_parts, *arrays, *before]
    return pl.pallas_call(
        functools.partial(grads_kernel, first),
        in_specs=[pl.BlockSpec(memory_space=pltpu.SMEM)] + [VMEM] * len(inputs),
        out_specs=[VMEM] * 2,
        out_shape=[pltpu.VMEM(half, jnp.bfloat16), pltpu.VMEM(whole, jnp.bfloat16)],
        scratch_shapes=[pltpu.VMEM((3 * stat_parts[0].shape[0], rows), jnp.float32)],
        compiler_params=PARAMS,
        cost_estimate=pl.CostEstimate(
            flops=8 * pairs * HD, bytes_accessed=2 * len(arrays) * half[0] * half[1], transcendentals=pairs
        ),
        name="grads",
    )(replica, *map(in_vmem, inputs))


def call_spread(layer_input, places):
    rows, features = layer_input.shape
    return pl.pallas_call(
        spread_kernel,
        in_specs=[ANY],
        out_specs=ANY,
        out_shape=jax.ShapeDtypeStruct((places * rows, features // places), jnp.bfloat16),
        scratch_shapes=[pltpu.SemaphoreType.DMA((places,))],
        compiler_params=PARAMS,
        cost_estimate=pl.CostEstimate(flops=0, bytes_accessed=4 * rows * features, transcendentals=0),
        name="spread",
    )(layer_input)


def call_weight(half, features, mine, columns, pieces, held, saved):
    part = pieces[0].shape[1]
    blocks = part // WIDE
    tokens, width = columns.shape
    inputs = [columns, *pieces, *saved]
    return pl.pallas_call(
        functools.partial(weight_kernel, bool(saved)),
        grid=(blocks,),
        in_specs=[pl.BlockSpec(memory_space=pltpu.SMEM)] + [VMEM] * len(inputs) + [ANY] * len(held),
        out_specs=[pl.BlockSpec((width, WIDE), lambda step: (0, step + half * blocks))] + [ANY] * len(saved),
        out_shape=[jax.ShapeDtypeStruct((width, features), jnp.bfloat16)]
        + [jax.ShapeDtypeStruct(array.shape, array.dtype) for array in saved],
        scratch_shapes=[
            pltpu.VMEM((width, tokens), jnp.bfloat16),
            pltpu.VMEM((tokens, WIDE), jnp.bfloat16),
            pltpu.SemaphoreType.DMA,
        ],
        input_output_aliases={1 + len(inputs): 0} if held else {},
        compiler_params=PARAMS,
        cost_estimate=pl.CostEstimate(
            flops=2 * width * tokens * part, bytes_accessed=2 * part * (tokens + width), transcendentals=0
        ),
        name="weight",
    )(mine, *map(in_vmem, inputs), *held)


def local(layer_input, queries, key_vectors, value_vectors, output_grad, partner_offsets):
    rows, features = queries.shape
    steps = features // (HD * STEP)
    docs = len(DOCS)
    places = lax.axis_size("fsdp")
    mine = lax.axis_index("fsdp").astype(jnp.int32).reshape(1)
    replica = lax.axis_index("dp").astype(jnp.int32).reshape(1)
    queries, mine, replica = lax.optimization_barrier((queries, mine, replica))

    others = [traded(array, "dp", 1, True) for array in (queries, output_grad)]
    firsts = [traded(array, "dp", 1, False) for array in (queries, output_grad)]
    near = list(zip(firsts, others))
    seconds = [traded(first, "dp", 1, True) for first in firsts]
    far = list(zip([traded(other, "dp", 1, False) for other in others], seconds))
    query_docs, grad_docs = (
        [array, *near[at], *far[at]] for at, array in enumerate((queries, output_grad))
    )

    own = [key_vectors, value_vectors]
    stats = call_stats(0, NEAR, partner_offsets, own + query_docs[:NEAR] + grad_docs[:NEAR], [])
    columns = call_spread(layer_input, places)
    stats, columns = lax.optimization_barrier((stats, columns))
    columns = lax.all_to_all(columns, "fsdp", 0, 0, tiled=True)
    stats = call_stats(NEAR, docs, partner_offsets, own + query_docs[NEAR:] + grad_docs[NEAR:], [stats])

    replicas = lax.axis_size("dp")
    groups = [list(range(low, low + GROUP)) for low in range(0, replicas, GROUP)]
    here = lax.all_to_all(stats, "dp", 0, 0, axis_index_groups=groups, tiled=True)
    after_odd = traded(here, "dp", GROUP, True)
    here, columns = lax.optimization_barrier((here, columns))
    stat_parts = [after_odd, here, traded(here, "dp", GROUP, False)]

    each = steps // HALVES
    arrays = own + query_docs + grad_docs
    halves, values = [], []
    for half in range(HALVES):
        key_half, value_part = call_grads(half * each, each, replica, stat_parts, arrays, values)
        halves.append(key_half)
        values = [value_part]

    for half, key_half in enumerate(halves):
        across = swapped(key_half, "fsdp", 2)
        pieces = [key_half, swapped(key_half, "fsdp", 1), across, swapped(across, "fsdp", 1)]
        if half == 0:
            weight, value_grad = call_weight(half, features, mine, columns, pieces, [], values)
        else:
            (weight,) = call_weight(half, features, mine, columns, pieces, [weight], [])
    return weight[None], value_grad


def solution(mesh):
    return jax.shard_map(
        local,
        mesh=mesh,
        in_specs=(
            P(("dp", "fsdp"), None),
            P(("dp", "fsdp"), None),
            P(("dp", "fsdp"), None),
            P(("dp", "fsdp"), None),
            P(("dp", "fsdp"), None),
            P("dp", None),
        ),
        out_specs=(P("dp", "fsdp", None), P(("dp", "fsdp"), None)),
        check_vma=False,
    )
```

```python
import functools

import jax
import jax.numpy as jnp
from jax import lax
from jax.experimental import pallas as pl
from jax.experimental.pallas import tpu as pltpu
from jax.sharding import PartitionSpec as P

HD = 128
DOCS = (0, 1, -1, 2, -2)
GROUP = 4
STEP = 4
TILE = 8
NEAR = 3
HALVES = 2
WIDE = 512
VMEM = pl.BlockSpec(memory_space=pltpu.VMEM)
ANY = pl.BlockSpec(memory_space=pl.ANY)
PARAMS = pltpu.CompilerParams(vmem_limit_bytes=24 << 20)
FAR = 1e30


def traded(value, axis, size, odd):
    count = lax.axis_size(axis)
    blocks = count // size
    pairs = []
    for source in range(count):
        block = source // size
        step = 1 if (block % 2 == 1) == odd else -1
        pairs.append((source, (block + step) % blocks * size + source % size))
    return lax.ppermute(value, axis, pairs)


def swapped(value, axis, mask):
    pairs = [(source, source ^ mask) for source in range(lax.axis_size(axis))]
    return lax.ppermute(value, axis, pairs)


def dot_nt(a, b):
    return lax.dot_general(a, b, (((1,), (1,)), ((), ())), preferred_element_type=jnp.float32)


def dot_nn(a, b):
    return lax.dot_general(a, b, (((1,), (0,)), ((), ())), preferred_element_type=jnp.float32)


def scores_of(keys, query_rows, own_first):
    scores = dot_nt(keys, query_rows) * (HD ** (-0.5))
    if not own_first:
        return scores
    rows = keys.shape[0]
    own = scores[:, :rows]
    key_at = lax.broadcasted_iota(jnp.int32, own.shape, 0)
    query_at = lax.broadcasted_iota(jnp.int32, own.shape, 1)
    own = jnp.where(key_at <= query_at, own, -FAR)
    return jnp.concatenate([own, scores[:, rows:]], 1)


def in_vmem(array):
    return pltpu.with_memory_space_constraint(array, pltpu.VMEM)


def head_rows(refs, cols):
    return jnp.concatenate([ref[:, cols] for ref in refs], 0)


def stats_kernel(low, offsets_ref, keys_ref, values_ref, *refs):
    count = (len(refs) - 1) // 2
    query_refs, grad_refs, out_ref = refs[:count], refs[count : 2 * count], refs[-1]
    rows, features = keys_ref.shape
    steps = features // (STEP * HD)

    def group(step, carry):
        base = pl.multiple_of(step * TILE, TILE)
        for head in range(STEP):
            cols = pl.ds(pl.multiple_of((step * STEP + head) * HD, HD), HD)
            scores = scores_of(keys_ref[:, cols], head_rows(query_refs, cols), low == 0)
            prob_grad = dot_nt(values_ref[:, cols], head_rows(grad_refs, cols))
            top = jnp.max(scores, 0, keepdims=True)
            weights = jnp.exp(scores - top)
            total = jnp.sum(weights, 0, keepdims=True)
            mean = jnp.sum(weights * prob_grad, 0, keepdims=True) / total
            lse = top + jnp.log(total)
            for doc in range(count):
                cut = slice(doc * rows, (doc + 1) * rows)
                start = base + (low + doc) * steps * TILE
                out_ref[pl.ds(start + head, 1), :] = lse[:, cut]
                out_ref[pl.ds(start + STEP + head, 1), :] = mean[:, cut]
        return carry

    lax.fori_loop(0, steps, group, 0)
    if low:
        before_ref = refs[2 * count]
        each = out_ref.shape[0] // GROUP
        out_ref[: before_ref.shape[0], :] = before_ref[...]
        for slot in range(2):
            value = offsets_ref[0, slot].astype(jnp.float32)
            at = each - TILE + slot * STEP
            out_ref[at : at + STEP, :] = jnp.full((STEP, rows), value, jnp.float32)
        for copy in range(1, GROUP):
            out_ref[copy * each : (copy + 1) * each, :] = out_ref[:each, :]


def merged(stat_ref, me, step, steps):
    stride = stat_ref.shape[0] // (3 * GROUP)
    sign = 1 - 2 * (me % 2)
    sign_real = sign.astype(jnp.float32)

    def tile(hops, row):
        place = me + GROUP + sign * hops
        return stat_ref[pl.ds(pl.multiple_of(place * stride + row, TILE), TILE), :]

    lse_rows, delta_rows = [], []
    for doc in DOCS:
        offsets = tile(doc, stride - TILE) * sign_real
        first, second = offsets[:STEP], offsets[STEP:]
        parts = []
        for hop in DOCS:
            name = -hop if (doc + hop) % 2 == 0 else hop
            stat = tile(doc + hop, (DOCS.index(name) * steps + step) * TILE)
            lse, mean = stat[:STEP], stat[STEP:]
            if hop:
                lse = jnp.where((first == hop) | (second == hop), lse, -FAR)
            parts.append((lse, mean))
        top = functools.reduce(jnp.maximum, [lse for lse, _ in parts])
        weights = [jnp.exp(lse - top) for lse, _ in parts]
        total = sum(weights)
        delta = sum(weight * mean for weight, (_, mean) in zip(weights, parts)) / total
        lse = top + jnp.log(total)
        if doc:
            lse = jnp.where((first == -doc) | (second == -doc), lse, FAR)
        lse_rows.append(lse)
        delta_rows.append(delta)
    return jnp.concatenate(lse_rows, 1), jnp.concatenate(delta_rows, 1)


def grads_kernel(first, replica_ref, *refs):
    count = len(DOCS)
    stat_refs, (keys_ref, values_ref), refs = refs[:3], refs[3:5], refs[5:]
    query_refs, grad_refs = refs[:count], refs[count : 2 * count]
    key_half, value_out, stat_ref = refs[-3:]
    skip = value_out.shape[1] - key_half.shape[1]
    if skip:
        value_out[:, :skip] = refs[-4][...]
    half = key_half.shape[1]
    each = half // (STEP * HD)
    steps = keys_ref.shape[1] // (STEP * HD)
    size = stat_refs[0].shape[0]
    replica = replica_ref[0]

    above = 2 - 2 * (replica // GROUP % 2)
    for place, ref in zip((2 - above, 1, above), stat_refs):
        stat_ref[pl.ds(pl.multiple_of(place * size, TILE), size), :] = ref[...]

    def group(at, carry):
        step = at + first
        lse, delta = merged(stat_ref, replica % GROUP, step, steps)
        for head in range(STEP):
            cols = pl.ds(pl.multiple_of((step * STEP + head) * HD, HD), HD)
            out_cols = pl.ds(pl.multiple_of((at * STEP + head) * HD, HD), HD)
            query_rows = jnp.concatenate([query_refs[0][:, cols], head_rows(query_refs[1:], out_cols)], 0)
            grad_rows = jnp.concatenate([grad_refs[0][:, cols], head_rows(grad_refs[1:], out_cols)], 0)
            scores = scores_of(keys_ref[:, cols], query_rows, True)
            prob_grad = dot_nt(values_ref[:, cols], grad_rows)
            probs = jnp.exp(scores - lse[head : head + 1])
            score_grad = probs * (prob_grad - delta[head : head + 1]) * (HD ** (-0.5))
            key_total = dot_nn(score_grad.astype(jnp.bfloat16), query_rows)
            value_total = dot_nn(probs.astype(jnp.bfloat16), grad_rows)
            key_half[:, out_cols] = key_total.astype(jnp.bfloat16)
            value_cols = pl.ds(pl.multiple_of(skip + (at * STEP + head) * HD, HD), HD)
            value_out[:, value_cols] = value_total.astype(jnp.bfloat16)
        return carry

    lax.fori_loop(0, each, group, 0)


def spread_kernel(input_ref, out_ref, sems):
    rows, features = input_ref.shape
    width = out_ref.shape[1]
    copies = [
        pltpu.make_async_copy(
            input_ref.at[:, pl.ds(place * width, width)], out_ref.at[pl.ds(place * rows, rows), :], sems.at[place]
        )
        for place in range(features // width)
    ]
    for copy in copies:
        copy.start()
    for copy in copies:
        copy.wait()


def weight_kernel(saves, mine_ref, inputs_ref, *refs):
    pieces, (turned_ref, grads_ref, sem) = refs[:4], refs[-3:]
    out_ref = refs[-5] if saves else refs[-4]
    wide = out_ref.shape[1]
    rows = pieces[0].shape[0]
    step = pl.program_id(0)
    copy = pltpu.make_async_copy(refs[4], refs[-4], sem) if saves else None

    @pl.when(step == 0)
    def _():
        if saves:
            copy.start()
        turned_ref[...] = inputs_ref[...].T

    cols = pl.ds(pl.multiple_of(step * wide, HD), wide)
    for k, ref in enumerate(pieces):
        place = pl.multiple_of((mine_ref[0] ^ k) * rows, rows)
        grads_ref[pl.ds(place, rows), :] = ref[:, cols]
    out_ref[...] = dot_nn(turned_ref[...], grads_ref[...]).astype(jnp.bfloat16)

    if saves:

        @pl.when(step == pl.num_programs(0) - 1)
        def _():
            copy.wait()


def call_stats(low, high, partner_offsets, arrays, before):
    rows, features = arrays[0].shape
    heads = features // HD
    docs = len(DOCS)
    out_rows = high * heads // STEP * TILE if high < docs else GROUP * (docs * heads // STEP + 1) * TILE
    pairs = rows * rows * heads * (high - low)
    return pl.pallas_call(
        functools.partial(stats_kernel, low),
        in_specs=[pl.BlockSpec(memory_space=pltpu.SMEM)] + [VMEM] * (len(arrays) + len(before)),
        out_specs=VMEM,
        out_shape=pltpu.VMEM((out_rows, rows), jnp.float32),
        compiler_params=PARAMS,
        cost_estimate=pl.CostEstimate(
            flops=4 * pairs * HD, bytes_accessed=2 * len(arrays) * rows * features, transcendentals=pairs
        ),
        name="stats",
    )(partner_offsets, *map(in_vmem, arrays), *map(in_vmem, before))


def call_grads(first, each, replica, stat_parts, own, query_docs, grad_docs, before):
    rows, features = own[0].shape
    count = len(query_docs)
    pairs = rows * rows * count * each * STEP
    half = (rows, each * STEP * HD)
    whole = (rows, (len(before) + 1) * half[1])
    block = pl.BlockSpec(half, lambda step: (0, first // each))
    docs = [VMEM] + [block] * (count - 1)
    return pl.pallas_call(
        functools.partial(grads_kernel, first),
        grid=(1,),
        in_specs=[pl.BlockSpec(memory_space=pltpu.SMEM)]
        + [VMEM] * (len(stat_parts) + len(own))
        + docs * 2
        + [VMEM] * len(before),
        out_specs=[VMEM] * 2,
        out_shape=[pltpu.VMEM(half, jnp.bfloat16), pltpu.VMEM(whole, jnp.bfloat16)],
        scratch_shapes=[pltpu.VMEM((3 * stat_parts[0].shape[0], rows), jnp.float32)],
        compiler_params=PARAMS,
        cost_estimate=pl.CostEstimate(
            flops=8 * pairs * HD,
            bytes_accessed=2 * (2 + 2 * count) * half[0] * half[1],
            transcendentals=pairs,
        ),
        name="grads",
    )(
        replica,
        *map(in_vmem, [*stat_parts, *own]),
        in_vmem(query_docs[0]),
        *query_docs[1:],
        in_vmem(grad_docs[0]),
        *grad_docs[1:],
        *map(in_vmem, before),
    )


def call_spread(layer_input, places):
    rows, features = layer_input.shape
    return pl.pallas_call(
        spread_kernel,
        in_specs=[ANY],
        out_specs=ANY,
        out_shape=jax.ShapeDtypeStruct((places * rows, features // places), jnp.bfloat16),
        scratch_shapes=[pltpu.SemaphoreType.DMA((places,))],
        compiler_params=PARAMS,
        cost_estimate=pl.CostEstimate(flops=0, bytes_accessed=4 * rows * features, transcendentals=0),
        name="spread",
    )(layer_input)


def call_weight(half, features, mine, columns, pieces, held, saved):
    part = pieces[0].shape[1]
    blocks = part // WIDE
    tokens, width = columns.shape
    inputs = [columns, *pieces, *saved]
    return pl.pallas_call(
        functools.partial(weight_kernel, bool(saved)),
        grid=(blocks,),
        in_specs=[pl.BlockSpec(memory_space=pltpu.SMEM)] + [VMEM] * len(inputs) + [ANY] * len(held),
        out_specs=[pl.BlockSpec((width, WIDE), lambda step: (0, step + half * blocks))] + [ANY] * len(saved),
        out_shape=[jax.ShapeDtypeStruct((width, features), jnp.bfloat16)]
        + [jax.ShapeDtypeStruct(array.shape, array.dtype) for array in saved],
        scratch_shapes=[
            pltpu.VMEM((width, tokens), jnp.bfloat16),
            pltpu.VMEM((tokens, WIDE), jnp.bfloat16),
            pltpu.SemaphoreType.DMA,
        ],
        input_output_aliases={1 + len(inputs): 0} if held else {},
        compiler_params=PARAMS,
        cost_estimate=pl.CostEstimate(
            flops=2 * width * tokens * part, bytes_accessed=2 * part * (tokens + width), transcendentals=0
        ),
        name="weight",
    )(mine, *map(in_vmem, inputs), *held)


def local(layer_input, queries, key_vectors, value_vectors, output_grad, partner_offsets):
    rows, features = queries.shape
    steps = features // (HD * STEP)
    docs = len(DOCS)
    places = lax.axis_size("fsdp")
    mine = lax.axis_index("fsdp").astype(jnp.int32).reshape(1)
    replica = lax.axis_index("dp").astype(jnp.int32).reshape(1)
    queries, mine, replica = lax.optimization_barrier((queries, mine, replica))

    others = [traded(array, "dp", 1, True) for array in (queries, output_grad)]
    firsts = [traded(array, "dp", 1, False) for array in (queries, output_grad)]
    near = list(zip(firsts, others))
    seconds = [traded(first, "dp", 1, True) for first in firsts]
    far = list(zip([traded(other, "dp", 1, False) for other in others], seconds))
    query_docs, grad_docs = (
        [array, *near[at], *far[at]] for at, array in enumerate((queries, output_grad))
    )

    own = [key_vectors, value_vectors]
    stats = call_stats(0, NEAR, partner_offsets, own + query_docs[:NEAR] + grad_docs[:NEAR], [])
    columns = call_spread(layer_input, places)
    stats, columns = lax.optimization_barrier((stats, columns))
    columns = lax.all_to_all(columns, "fsdp", 0, 0, tiled=True)
    stats = call_stats(NEAR, docs, partner_offsets, own + query_docs[NEAR:] + grad_docs[NEAR:], [stats])

    replicas = lax.axis_size("dp")
    groups = [list(range(low, low + GROUP)) for low in range(0, replicas, GROUP)]
    here = lax.all_to_all(stats, "dp", 0, 0, axis_index_groups=groups, tiled=True)
    after_odd = traded(here, "dp", GROUP, True)
    here, columns = lax.optimization_barrier((here, columns))
    stat_parts = [after_odd, here, traded(here, "dp", GROUP, False)]

    each = steps // HALVES
    halves, values = [], []
    for half in range(HALVES):
        key_half, value_part = call_grads(half * each, each, replica, stat_parts, own, query_docs, grad_docs, values)
        halves.append(key_half)
        values = [value_part]

    for half, key_half in enumerate(halves):
        across = swapped(key_half, "fsdp", 2)
        pieces = [key_half, swapped(key_half, "fsdp", 1), across, swapped(across, "fsdp", 1)]
        if half == 0:
            weight, value_grad = call_weight(half, features, mine, columns, pieces, [], values)
        else:
            (weight,) = call_weight(half, features, mine, columns, pieces, [weight], [])
    return weight[None], value_grad


def solution(mesh):
    return jax.shard_map(
        local,
        mesh=mesh,
        in_specs=(
            P(("dp", "fsdp"), None),
            P(("dp", "fsdp"), None),
            P(("dp", "fsdp"), None),
            P(("dp", "fsdp"), None),
            P(("dp", "fsdp"), None),
            P("dp", None),
        ),
        out_specs=(P("dp", "fsdp", None), P(("dp", "fsdp"), None)),
        check_vma=False,
    )
```
